32 devices in a mesh: seq: 8 (over y, x, core), head: 4 (over z).
Axes of the slice: x: 2, y: 2, z: 4, core: 2. Of those that a mesh axis runs over, the one named last changes fastest.
Arguments:
- signal: bfloat16 [1024, 8192], P('seq', 'head'), may hold values from -6 to 6
- gate_input: bfloat16 [1024, 8192], P('seq', 'head'), may hold values from -6 to 6
- state_in: bfloat16 [1024, 128], P('seq'), may hold values from -1.796875 to 1.796875
- state_out: bfloat16 [1024, 128], P('seq'), may hold values from -1.796875 to 1.796875
- step_size: float32 [128, 1024], P('head', 'seq'), may hold values from 0 to 2, as said below
- log_decay: float32 [128, 1024], P('head', 'seq'), may hold values from -4 to 0, as said below
- skip_gain: float32 [128], P('head'), may hold values from 0.5 to 1.5
- norm_gain: float32 [8192], P('head'), may hold values from 0.1 to 1.9
- out_weight: bfloat16 [8192, 4096], P('head', 'seq'), may hold values from -0.09375 to 0.09375
Outputs:
- mixed: bfloat16 [1024, 4096], P('seq', 'head')
The draws below stay inside these ranges and needn't reach their ends.
Inputs may be any that keep to these rules, and one draw needn't show every extreme that they name: step_size is positive. log_decay is negative.
All inputs are finite; a program needn't handle non-finite values.
Results may differ from the reference program's by a relative error of at most 0.025.
Values may be sent and summed in bfloat16 or wider, within the bound.
No kernel may reach another device: no remote copies, remote signals or barrier semaphores. Data moves between devices by JAX's collectives and lax.ppermute only.
A program may use at most 64 MiB of HBM per device.

```python
import math
import jax
import jax.numpy as jnp
from jax import lax

D = 4096
HEADS = 128
HEAD_DIM = 64
STATE = 128
SEQ = 1024
INNER = 8192
N_HEAD = 4


def head_rates(key):
    base = jax.random.fold_in(key, 7)
    pick = jax.random.uniform(jax.random.fold_in(base, 1), (HEADS,))
    slow_share = 0.5
    slow = jnp.exp(jax.random.uniform(jax.random.fold_in(base, 2), (HEADS,), jnp.float32, math.log(0.2 / SEQ), math.log(2.0 / SEQ)))
    fast = jnp.exp(jax.random.uniform(jax.random.fold_in(base, 3), (HEADS,), jnp.float32, math.log(1.0 / 50.0), math.log(1.0 / 8.0)))
    return jnp.where(pick < slow_share, slow, fast)


def draw_log_decay(key, part):
    decay_rates = head_rates(key)
    coarse_state = jax.random.uniform(jax.random.fold_in(key, 21), (HEADS, SEQ), jnp.float32, 0.5, 1.5)
    device_positions = jax.random.randint(jax.random.fold_in(key, 31), (4,), 0, SEQ)
    decay_amounts = jax.random.uniform(jax.random.fold_in(key, 41), (4,), jnp.float32, 0.2, 0.5)
    feature_column = jnp.arange(SEQ)[None, :]
    token_window = jnp.sum(jnp.where(feature_column == device_positions[:, None], jnp.log(1.0 - decay_amounts)[:, None], 0.0), axis=0)
    return (-decay_rates[:, None] * coarse_state + token_window[None, :]).astype(jnp.float32)


def draw_step_size(key, part):
    decay_rates = head_rates(key)
    ramp = 1.0 + 2.0 * jnp.arange(HEADS, dtype=jnp.float32) / max(HEADS - 1, 1)
    coarse_state = jax.random.uniform(jax.random.fold_in(key, 51), (HEADS, SEQ), jnp.float32, 0.5, 1.5)
    return (jnp.sqrt(decay_rates)[:, None] * ramp[:, None] * coarse_state).astype(jnp.float32)


def strengthened(values, stream_key, source, target, parts, factor):
    owner, partner = [(jnp.arange(values.shape[axis_at]) // (values.shape[axis_at] // parts)).reshape([-1 if axis == axis_at else 1 for axis in range(values.ndim)]) for axis_at in (source, target)]
    chosen = jax.random.permutation(stream_key, parts)[partner]
    strong = (owner == chosen) | (owner == (partner + parts // 2) % parts)
    return jnp.where(strong, factor * values, values)


def block_scale(key, dims, cuts, low, top_value):
    def one(position, blocks):
        heights = jax.random.uniform(jax.random.fold_in(jax.random.fold_in(key, 6), position), (blocks,), jnp.float32, low / len(cuts), top_value / len(cuts))
        return jnp.repeat(jnp.exp(heights), dims[position] // blocks).reshape((-1,) + (1,) * (len(dims) - position - 1))

    factor_of = one(*cuts[0])
    for cut in cuts[1:]:
        factor_of = factor_of * one(*cut)
    return factor_of


def centred(key, dims, deviation, most, split=(), kind=jnp.bfloat16):
    gain = block_scale(key, dims, split, -0.22, 0.18) if split else 1.0
    values = jax.random.normal(key, dims, jnp.float32) * deviation * gain
    return jnp.minimum(jnp.maximum(values, -most), most).astype(kind)


def noise_with(key, shape, scale, reach, shards, heavy, kind=jnp.bfloat16):
    array = scale * jax.random.normal(key, shape, jnp.float32)
    if shards:
        array = array * block_scale(key, shape, shards, -0.22, 0.18)
    return jnp.clip(strengthened(array, jax.random.fold_in(key, 3), *heavy), -reach, reach).astype(kind)


def setup_inputs(seed: int = 0) -> dict:
    keys = jax.random.split(jax.random.key(seed), 10)
    signal = centred(keys[0], (SEQ, INNER), 1.0, 6.0, ((0, 8), (1, 4)))
    gate_input = centred(keys[1], (SEQ, INNER), 1.0, 6.0, ((0, 8), (1, 4)))
    state_in = centred(keys[2], (SEQ, STATE), 0.3, 1.796875, ((0, 8),))
    state_out = centred(keys[3], (SEQ, STATE), 0.3, 1.796875, ((0, 8),))
    step_size = draw_step_size(jax.random.fold_in(keys[9], 71), 0)
    log_decay = draw_log_decay(jax.random.fold_in(keys[9], 71), 0)
    skip_gain = jnp.clip(0.5 + 1.0 * jax.random.uniform(keys[6], (HEADS,), jnp.float32) ** block_scale(keys[6], (HEADS,), ((0, 4),), -0.2, 0.2), 0.5, 1.5)
    norm_gain = jnp.clip(1.0 + 0.18 * jax.random.normal(keys[7], (INNER,), jnp.float32), 0.1, 1.9)
    out_weight = noise_with(keys[8], (INNER, D), INNER ** -0.5, 0.09375, ((0, 4), (1, 8)), (0, 1, 8, 2.0))
    return dict(signal=signal, gate_input=gate_input, state_in=state_in, state_out=state_out, step_size=step_size, log_decay=log_decay, skip_gain=skip_gain, norm_gain=norm_gain, out_weight=out_weight)


HIGH = lax.Precision.HIGHEST

def ssd_block(state, inputs):
    signal_part, keys_part, queries_part, decay_part, step_sizes_local = inputs
    signal_f = signal_part.astype(jnp.float32)
    keys_f = keys_part.astype(jnp.float32)
    queries_f = queries_part.astype(jnp.float32)
    running = jnp.cumsum(decay_part, axis=1)
    width = decay_part.shape[1]
    lower = (jnp.arange(width)[:, None] >= jnp.arange(width)[None, :])[None]
    spread = running[:, :, None] - running[:, None, :]
    factors = jnp.where(lower, jnp.exp(jnp.where(lower, spread, 0.0)), 0.0)
    scores = jnp.dot(queries_f, keys_f.T, precision=HIGH)
    weights = factors * scores[None] * step_sizes_local[:, None, :]
    inside = jnp.einsum('hij,jhp->ihp', weights, signal_f, precision=HIGH)
    carried = jnp.einsum('in,hpn->ihp', queries_f, state, precision=HIGH) * jnp.exp(running).T[:, :, None]
    tail = jnp.exp(running[:, -1:] - running) * step_sizes_local
    fresh = jnp.einsum('hj,jhp,jn->hpn', tail, signal_f, keys_f, precision=HIGH)
    new_state = jnp.exp(running[:, -1])[:, None, None] * state + fresh
    return (new_state, inside + carried)

def reference(signal, gate_input, state_in, state_out, step_size, log_decay, skip_gain, norm_gain, out_weight):
    width = min(256, SEQ)
    blocks = SEQ // width
    inputs = (signal.reshape(blocks, width, HEADS, HEAD_DIM), state_in.reshape(blocks, width, STATE), state_out.reshape(blocks, width, STATE), log_decay.reshape(HEADS, blocks, width).transpose(1, 0, 2), step_size.reshape(HEADS, blocks, width).transpose(1, 0, 2))
    start = jnp.zeros((HEADS, HEAD_DIM, STATE), jnp.float32)
    final_state, outputs = lax.scan(ssd_block, start, inputs)
    channels = signal.reshape(SEQ, HEADS, HEAD_DIM).astype(jnp.float32)
    result = outputs.reshape(SEQ, HEADS, HEAD_DIM) + skip_gain[None, :, None] * channels
    gated = result.reshape(SEQ, HEADS * HEAD_DIM) * jax.nn.silu(gate_input.astype(jnp.float32))
    meansq = lax.optimization_barrier(jnp.mean(gated * gated, axis=1, keepdims=True))
    hidden = (gated * lax.rsqrt(meansq + 1e-05) * norm_gain[None, :]).astype(jnp.bfloat16)
    group_width = HEADS * HEAD_DIM // N_HEAD
    total = jnp.zeros((SEQ, D), jnp.float32)
    for group in range(N_HEAD):
        lo_edge = group * group_width
        partial_sum = jnp.dot(hidden[:, lo_edge:lo_edge + group_width], out_weight[lo_edge:lo_edge + group_width], preferred_element_type=jnp.float32).astype(jnp.bfloat16)
        partial_sum = lax.optimization_barrier(partial_sum)
        total = total + partial_sum.astype(jnp.float32)
    return total.astype(jnp.bfloat16)
```

```python
import jax
import jax.numpy as jnp
from jax import lax
from jax.sharding import PartitionSpec as P

BOTH = ("seq", "head")


def split2(v):
    hi = v.astype(jnp.bfloat16)
    lo = (v - hi.astype(jnp.float32)).astype(jnp.bfloat16)
    return hi, lo


def body(n_chip, n_head, signal, gate_input, state_in, state_out, step_size, log_decay, skip_gain, norm_gain, out_weight):
    f32, bf16 = jnp.float32, jnp.bfloat16
    rows = signal.shape[0]
    heads = log_decay.shape[0]
    half = heads // 2
    wide = signal.shape[1] // 2
    size = signal.shape[1] // heads
    states = state_in.shape[1]
    k = lax.axis_index("seq") % 2
    sib = [(i, i ^ 1) for i in range(2 * n_chip)]

    def mine(a, axis):
        n = a.shape[axis] // 2
        return lax.dynamic_slice_in_dim(a, k * n, n, axis)

    def theirs(a, axis):
        n = a.shape[axis] // 2
        return lax.dynamic_slice_in_dim(a, (1 - k) * n, n, axis)

    def swap(a):
        return lax.ppermute(a, "seq", sib)

    def ordered(own, other):
        return jnp.where(k == 0, own, other), jnp.where(k == 0, other, own)

    rates = jnp.concatenate([step_size, log_decay], 0).reshape(2, heads, rows)
    first = jnp.concatenate([theirs(signal, 1), state_in], 1)
    got1 = swap(first)
    got_r = swap(theirs(rates, 1))
    second = jnp.concatenate([theirs(gate_input, 1), state_out], 1)
    got2 = swap(second)
    x2 = ordered(mine(signal, 1), got1[:, :wide])
    b2 = ordered(state_in, got1[:, wide:])
    z2 = ordered(mine(gate_input, 1), got2[:, :wide])
    c2 = ordered(state_out, got2[:, wide:])
    r2 = ordered(mine(rates, 1), got_r)

    def expand(v):
        return jnp.repeat(v.T, size, axis=1)

    part = []
    for x, b, r in zip(x2, b2, r2):
        dt, ld = r[0], r[1]
        run = jnp.cumsum(ld, axis=1)
        tail = jnp.exp(run[:, -1:] - run) * dt
        xs = (x.astype(f32) * expand(tail)).astype(bf16)
        st = lax.dot_general(b, xs, (((0,), (0,)), ((), ())), preferred_element_type=f32)
        part.append((run, st, jnp.exp(run[:, -1])))
    rep = lambda v: jnp.repeat(v, size)[None, :]
    chip_state = rep(part[1][2]) * part[0][1] + part[1][1]
    chip_decay = jnp.exp(part[0][0][:, -1] + part[1][0][:, -1])
    hi, lo = split2(rep(chip_decay))
    msg = jnp.concatenate([chip_state.astype(bf16), hi, lo, jnp.zeros((14, wide), bf16)], 0)
    got = [
        lax.ppermute(msg, "seq", [(s, s + 2 * j) for s in range(2 * n_chip - 2 * j)])
        for j in range(1, n_chip)
    ]
    y = []
    for (x, b, c, r, p) in zip(x2, b2, c2, r2, part):
        run, dt = p[0], r[0]
        scores = lax.dot_general(c, b, (((1,), (1,)), ((), ())), preferred_element_type=f32)
        lower = jnp.arange(rows)[:, None] >= jnp.arange(rows)[None, :]
        diff = jnp.where(lower, run[:, :, None] - run[:, None, :], -jnp.inf)
        w = (jnp.exp(diff) * scores[None] * dt[:, None, :]).astype(bf16)
        inside = jnp.einsum("hij,jhp->ihp", w, x.reshape(rows, half, size), preferred_element_type=f32)
        y.append(inside.reshape(rows, wide) + jnp.repeat(mine(skip_gain, 0), size)[None, :] * x.astype(f32))
    enter = jnp.zeros((states, wide), f32)
    for m in got[::-1]:
        f = m[states].astype(f32) + m[states + 1].astype(f32)
        enter = m[:states].astype(f32) + f[None, :] * enter
    enters = [enter, rep(part[0][2]) * enter + part[0][1]]
    gs, sq = [], []
    for yy, e, c, p, z in zip(y, enters, c2, part, z2):
        add = jnp.dot(c, e.astype(bf16), preferred_element_type=f32)
        yy = yy + add * expand(jnp.exp(p[0]))
        zf = z.astype(f32)
        gated = yy * zf / (1 + jnp.exp(-zf))
        sq.append(jnp.sum(gated * gated, axis=1))
        gs.append((gated * mine(norm_gain, 0)[None, :]).astype(bf16))
    tokens = 2 * rows
    sq = jnp.concatenate(sq)
    hi, lo = split2(sq)
    extra = jnp.pad(jnp.stack([hi, lo]), ((0, 14), (0, wide - tokens)))
    gmsg = jnp.concatenate(gs + [extra], 0)

    def pairs(f):
        out = []
        for s in range(2 * n_chip):
            for h in range(n_head):
                s2, h2 = f(s // 2, s % 2, h)
                out.append((s * n_head + h, s2 * n_head + h2))
        return out

    cols = out_weight.shape[1]
    z = []
    for m in range(n_head):
        across = pairs(lambda c, k, h: (2 * (c ^ h ^ m) + k, h))
        g1 = lax.ppermute(gmsg, BOTH, across)
        g2 = swap(g1)
        part_sum = jnp.dot(g1[:tokens], mine(out_weight, 0), preferred_element_type=f32)
        part_sum += jnp.dot(g2[:tokens], theirs(out_weight, 0), preferred_element_type=f32)
        sqs = g1[tokens:tokens + 2, :tokens].astype(f32) + g2[tokens:tokens + 2, :tokens].astype(f32)
        hi, lo = split2(sqs[0] + sqs[1])
        ext = jnp.zeros((16, cols), bf16)
        nrow = 2 * tokens // cols if 2 * tokens > cols else 1
        ext = jnp.concatenate([hi, lo]).reshape(nrow, -1)
        ext = jnp.pad(ext, ((0, 16 - nrow), (0, cols - ext.shape[1])))
        pmsg = jnp.concatenate([part_sum.astype(bf16), ext], 0)
        back = lax.ppermute(pmsg, BOTH, across)
        z.append(lax.ppermute(back, BOTH, pairs(lambda c, k, h: (2 * c + k, c ^ h ^ m))))
    total = sum(a[:tokens].astype(f32) for a in z)
    ss = sum(a[tokens:tokens + nrow].astype(f32).reshape(-1)[:2 * tokens] for a in z)
    ss = ss[:tokens] + ss[tokens:]
    scale = lax.rsqrt(ss / (2 * wide * n_head) + 1e-5)
    out = (total * scale[:, None]).astype(bf16)
    own, other = mine(out, 0), swap(theirs(out, 0))
    return jnp.concatenate(ordered(own, other), axis=1)


def solution(mesh):
    n_chip, n_head = mesh.shape["seq"] // 2, mesh.shape["head"]
    assert n_chip == n_head and n_head & (n_head - 1) == 0
    in_specs = (
        P("seq", "head"),
        P("seq", "head"),
        P("seq", None),
        P("seq", None),
        P("head", "seq"),
        P("head", "seq"),
        P("head"),
        P("head"),
        P("head", "seq"),
    )

    def run(*args):
        return body(n_chip, n_head, *args)

    return jax.shard_map(run, mesh=mesh, in_specs=in_specs, out_specs=P("seq", "head"), check_vma=False)
```

```python
import jax
import jax.numpy as jnp
from jax import lax
from jax.experimental import pallas as pl
from jax.experimental.pallas import tpu as pltpu
from jax.sharding import PartitionSpec as P

BOTH = ("seq", "head")
HIGH = lax.Precision.HIGHEST
f32, bf16 = jnp.float32, jnp.bfloat16
EXT = 16
VMEM_LIMIT = 48 * 1024 * 1024


def call(kernel, scalars, ins, in_specs, outs, out_specs, scratch=(), flops=0):
    moved = sum(a.size * a.dtype.itemsize for a in ins) + sum(
        o.size * o.dtype.itemsize for o in outs
    )
    return pl.pallas_call(
        kernel,
        out_shape=outs,
        grid_spec=pltpu.PrefetchScalarGridSpec(
            num_scalar_prefetch=1,
            grid=(1,),
            in_specs=in_specs,
            out_specs=out_specs,
            scratch_shapes=scratch,
        ),
        cost_estimate=pl.CostEstimate(flops=flops, bytes_accessed=moved, transcendentals=0),
        compiler_params=pltpu.CompilerParams(vmem_limit_bytes=VMEM_LIMIT),
    )(scalars, *ins)


def full(a):
    return pl.BlockSpec(a.shape, lambda i, s: (0,) * len(a.shape))


def lane_half(a):
    return pl.BlockSpec((a.shape[0], a.shape[1] // 2), lambda i, s: (0, s[0]))


def shape(dims, kind):
    return jax.ShapeDtypeStruct(dims, kind)


def nn(a, b, precision=None):
    return jnp.dot(a, b, preferred_element_type=f32, precision=precision)


def nt(a, b, precision=None):
    return lax.dot_general(a, b, (((1,), (1,)), ((), ())), preferred_element_type=f32, precision=precision)


def tn(a, b, precision=None):
    return lax.dot_general(a, b, (((0,), (0,)), ((), ())), preferred_element_type=f32, precision=precision)


def split2(v):
    hi = v.astype(bf16).astype(f32)
    return hi, v - hi


def half_rows(ref, k):
    v = ref[...]
    n = v.shape[0] // 2
    return jnp.where(k == 0, v[:n], v[n:])


def channel_map(heads, wide):
    head = lax.broadcasted_iota(jnp.int32, (heads, wide), 0)
    lane = lax.broadcasted_iota(jnp.int32, (heads, wide), 1)
    size = wide // heads
    return ((lane >= head * size) & (lane < (head + 1) * size)).astype(bf16)


def spread(v, spots):
    hi, lo = split2(v)
    return tn(hi.astype(bf16), spots) + tn(lo.astype(bf16), spots)


def ones_upto(rows):
    i = lax.broadcasted_iota(jnp.int32, (rows, rows), 0)
    j = lax.broadcasted_iota(jnp.int32, (rows, rows), 1)
    return (j <= i), (i <= j)


def state_kernel(s, xo, xr, bo, br, dto, dtr, ldo, ldr, msg, first):
    k = s[0]
    rows, wide = xo.shape
    _, upper = ones_upto(rows)
    got = []
    for x, b, dt, ld in ((xo, bo, dto, ldo), (xr, br, dtr, ldr)):
        dt, ld = half_rows(dt, k), half_rows(ld, k)
        spots = channel_map(ld.shape[0], wide)
        run = nn(ld, upper.astype(f32), HIGH)
        last = run[:, rows - 1 :]
        tail = jnp.exp(last - run) * dt
        scaled = (x[...].astype(f32) * spread(tail, spots)).astype(bf16)
        state = tn(b[...], scaled)
        decay = spread(jnp.exp(jnp.broadcast_to(last, (last.shape[0], 8))), spots)
        got.append((state, decay))
    (so, do), (sr, dr) = got
    even = k == 0
    s1, s2 = jnp.where(even, so, sr), jnp.where(even, sr, so)
    d2 = jnp.where(even, dr, do)
    n = s1.shape[0]
    msg[:n] = (d2[:1] * s1 + s2).astype(bf16)
    hi, lo = split2(do * dr)
    msg[n:] = jnp.concatenate([hi, lo], 0).astype(bf16)
    first[...] = s1


def unpack(ref):
    n = ref.shape[0] - EXT
    ext = ref[n:].astype(f32)
    return ref[:n].astype(f32), ext[:8] + ext[8:]


def join_kernel(s, own, other, out, *, bit):
    later = (s[1] >> bit) & 1 == 1
    so, do = unpack(own)
    st, dt = unpack(other)
    n = so.shape[0]
    s1, s2 = jnp.where(later, st, so), jnp.where(later, so, st)
    d2 = jnp.where(later, do, dt)
    out[:n] = (d2[:1] * s1 + s2).astype(bf16)
    hi, lo = split2(do * dt)
    out[n:] = jnp.concatenate([hi, lo], 0).astype(bf16)


def inside_kernel(s, xo, xr, bo, br, co, cr, dto, dtr, ldo, ldr, skip, out):
    k = s[0]
    rows, wide = xo.shape
    low, upper = ones_upto(rows)
    for turn, (x, b, c, dt, ld) in enumerate(((xo, bo, co, dto, ldo), (xr, br, cr, dtr, ldr))):
        start = pl.multiple_of(jnp.where(k == turn, 0, rows), rows)
        dt, ld = half_rows(dt, k), half_rows(ld, k)
        heads = ld.shape[0]
        size = wide // heads
        run = nn(ld, upper.astype(f32), HIGH)
        down = nt(low.astype(f32), ld, HIGH)
        scores = jnp.where(low, nt(c[...], b[...]), 0.0)
        lane = lax.broadcasted_iota(jnp.int32, (rows, 2 * size), 1)
        for pair in range(heads // 2):
            w = []
            for h in (2 * pair, 2 * pair + 1):
                gap = jnp.minimum(down[:, h : h + 1] - run[h : h + 1, :], 0.0)
                w.append((jnp.exp(gap) * scores * dt[h : h + 1, :]).astype(bf16))
            xp = x[:, 2 * pair * size : 2 * (pair + 1) * size]
            zero = jnp.zeros_like(xp)
            both = jnp.concatenate([jnp.where(lane < size, xp, zero), jnp.where(lane < size, zero, xp)], 0)
            y = nn(jnp.concatenate(w, 1), both)
            at = slice(2 * pair * size, 2 * (pair + 1) * size)
            out[pl.ds(start, rows), at] = y + skip[:, at] * xp.astype(f32)


def gate_kernel(s, inside, first, co, cr, ldo, ldr, zo, zr, gain, *rest):
    *states, out = rest
    k = s[0]
    rows, wide = zo.shape
    _, upper = ones_upto(rows)
    even = k == 0
    enter, through = jnp.zeros_like(first[...]), None
    for bit, ref in enumerate(states):
        st, dec = unpack(ref)
        dec = dec[:1]
        later = (s[1] >> bit) & 1 == 1
        add = st if through is None else st * through
        enter = enter + jnp.where(later, add, 0.0)
        dec = jnp.where(later, dec, 1.0)
        through = dec if through is None else through * dec
    ld1 = jnp.where(even, half_rows(ldo, k), half_rows(ldr, k))
    ld2 = jnp.where(even, half_rows(ldr, k), half_rows(ldo, k))
    c1, c2 = jnp.where(even, co[...], cr[...]), jnp.where(even, cr[...], co[...])
    spots = channel_map(ld1.shape[0], wide)
    ones = jnp.ones((8, wide), bf16)
    for turn, (c, ld) in enumerate(((c1, ld1), (c2, ld2))):
        run = nn(ld, upper.astype(f32), HIGH)
        decays = spread(jnp.exp(run), spots)
        carried = nn(c, enter.astype(bf16)) * decays
        y = inside[turn * rows : (turn + 1) * rows] + carried
        zf = (jnp.where(even, zo[...], zr[...]) if turn == 0 else jnp.where(even, zr[...], zo[...])).astype(f32)
        gated = y * zf / (1.0 + jnp.exp(-zf))
        sq_hi, sq_lo = split2(gated * gated)
        sq = nt(ones, sq_hi.astype(bf16)) + nt(ones, sq_lo.astype(bf16))
        base = turn * (rows + EXT)
        out[base : base + rows] = (gated * gain[...]).astype(bf16)
        hi, lo = split2(sq)
        ext = jnp.concatenate([hi, lo], 0)
        if wide > rows:
            ext = jnp.concatenate([ext, jnp.zeros((EXT, wide - rows), f32)], 1)
        out[base + rows : base + rows + EXT] = ext.astype(bf16)
        if turn == 0:
            enter = decays[rows - 1 : rows] * enter + first[...]


def project_kernel(s, *refs):
    *g, w, out = refs
    k = s[0]
    parts = len(g) // 2
    step = g[0].shape[0] * parts // 2
    rows = step - EXT
    depth = g[0].shape[1]
    here = pl.ds(pl.multiple_of(k * depth, depth), depth)
    there = pl.ds(pl.multiple_of((1 - k) * depth, depth), depth)
    ext = []
    for turn in range(2):
        if parts == 1:
            a, b, base = g[0], g[1], turn * step
        else:
            a, b, base = g[turn], g[2 + turn], 0
        got = nn(a[base : base + rows], w[here]) + nn(b[base : base + rows], w[there])
        out[turn * rows : (turn + 1) * rows] = got.astype(bf16)
        at = slice(base + rows, base + rows + EXT)
        e = a[at, :rows].astype(f32) + b[at, :rows].astype(f32)
        hi, lo = split2(e[:4] + e[8:12])
        ext += [hi, lo]
    ext = jnp.concatenate(ext, 0)
    cols = out.shape[1]
    if cols > rows:
        ext = jnp.concatenate([ext, jnp.zeros((EXT, cols - rows), f32)], 1)
    out[2 * rows :] = ext.astype(bf16)


def choose_kernel(s, *refs):
    n = (len(refs) - 1) // 2
    ins, outs, sem = refs[:n], refs[n : 2 * n], refs[2 * n]
    for m in range(n):
        for j in range(n):

            @pl.when((s[2] ^ m) == j)
            def _():
                pltpu.make_async_copy(ins[j], outs[m], sem.at[m]).start()

    for m in range(n):
        pltpu.make_async_copy(ins[0], outs[m], sem.at[m]).wait()


def sum_kernel(s, *refs, inner):
    *z, mine, theirs = refs
    k = s[0]
    rows = mine.shape[0]
    ext = sum(a[2 * rows :, :rows].astype(f32) for a in z)
    i = lax.broadcasted_iota(jnp.int32, (rows, rows), 0)
    j = lax.broadcasted_iota(jnp.int32, (rows, rows), 1)
    done = []
    for turn in range(2):
        e = ext[turn * 8 : turn * 8 + 8]
        sq = e[:1] + e[4:5]
        row = lax.rsqrt(sq / inner + 1e-5)
        col = jnp.sum(jnp.where(i == j, jnp.broadcast_to(row, (rows, rows)), 0.0), axis=1, keepdims=True)
        total = sum(a[turn * rows : (turn + 1) * rows].astype(f32) for a in z)
        done.append((total * col).astype(bf16))
    even = k == 0
    mine[...] = jnp.where(even, done[0], done[1])
    theirs[...] = jnp.where(even, done[1], done[0])


def body(n, n_head, signal, gate_input, state_in, state_out, step_size, log_decay, skip_gain, norm_gain, out_weight):
    rows = signal.shape[0]
    heads = log_decay.shape[0]
    wide = signal.shape[1] // 2
    size = signal.shape[1] // heads
    states = state_in.shape[1]
    cols = out_weight.shape[1]
    place, z = lax.axis_index("seq"), lax.axis_index("head")
    k, chip = place % 2, place // 2
    s = jnp.stack([k, chip, chip ^ z]).astype(jnp.int32)

    def swap(a):
        return lax.ppermute(a, "seq", [(i, i ^ 1) for i in range(2 * n)])

    def across(a, j):
        return lax.ppermute(a, "seq", [(i, i ^ (2 * j)) for i in range(2 * n)])

    x2, b2 = swap(signal), swap(state_in)
    dt2, ld2 = swap(step_size), swap(log_decay)
    z2, c2 = swap(gate_input), swap(state_out)
    skip = jnp.repeat(skip_gain, size).reshape(1, 2 * wide)
    gain = norm_gain.reshape(1, 2 * wide)

    ins = (signal, x2, state_in, b2, step_size, dt2, log_decay, ld2)
    specs = [lane_half(signal)] * 2 + [full(state_in)] * 2 + [full(step_size)] * 4
    msg_shape = shape((states + EXT, wide), bf16)
    first_shape = shape((states, wide), f32)
    msg, first = call(state_kernel, s, ins, specs, [msg_shape, first_shape], [full(msg_shape), full(first_shape)])
    got = []
    bits = n.bit_length() - 1
    for bit in range(bits):
        step = 1 << bit
        pairs = [(i, i ^ (2 * step)) for i in range(2 * n)]
        if bit == bits - 1:
            pairs = [p for p in pairs if p[1] > p[0]]
        new = lax.ppermute(msg, "seq", pairs)
        got.append(new)
        if bit == 0:
            ins = (signal, x2, state_in, b2, state_out, c2, step_size, dt2, log_decay, ld2, skip)
            specs = [lane_half(signal)] * 2 + [full(state_in)] * 4 + [full(step_size)] * 4 + [lane_half(skip)]
            inside_shape = shape((2 * rows, wide), f32)
            (inside,) = call(inside_kernel, s, ins, specs, [inside_shape], [full(inside_shape)])
        if bit < bits - 1:

            def join(*refs, bit=bit):
                join_kernel(*refs, bit=bit)

            (msg,) = call(join, s, (msg, new), [full(msg)] * 2, [msg_shape], [full(msg_shape)])

    ins = (inside, first, state_out, c2, log_decay, ld2, gate_input, z2, gain, *got)
    specs = [full(inside), full(first), full(state_out), full(c2), full(log_decay), full(ld2)]
    specs += [lane_half(gate_input)] * 2 + [lane_half(gain)] + [full(m) for m in got]
    g_shape = shape((2 * (rows + EXT), wide), bf16)
    (g,) = call(gate_kernel, s, ins, specs, [g_shape], [full(g_shape)])

    p_shape = shape((2 * rows + EXT, cols), bf16)

    def project(*g):
        ins = (*g, *[swap(a) for a in g], out_weight)
        return call(project_kernel, s, ins, [full(a) for a in ins], [p_shape], [full(p_shape)])[0]

    hidden = [(g,)] + [None] * (n - 1)
    if n == 4:
        gx, gy = across(g, 1), across(g, 2)
        hidden[1], hidden[2] = (gx,), (gy,)
        hidden[3] = (across(gx[: rows + EXT], 2), across(gy[rows + EXT :], 1))
    else:
        for j in range(1, n):
            hidden[j] = (across(g, j),)
    blocks = [project(*hidden[j]) for j in range(n)]
    blocks = [blocks[0]] + [across(blocks[j], j) for j in range(1, n)]

    any_spec = pl.BlockSpec(memory_space=pl.ANY)
    blocks = call(
        choose_kernel, s, blocks, [any_spec] * n, [p_shape] * n, [any_spec] * n,
        scratch=[pltpu.SemaphoreType.DMA((n,))],
    )
    blocks = [blocks[0]] + [
        lax.ppermute(blocks[m], "head", [(i, i ^ m) for i in range(n)]) for m in range(1, n)
    ]
    half = shape((rows, cols), bf16)

    def add(*refs):
        sum_kernel(*refs, inner=2 * wide * n_head)

    mine, theirs = call(add, s, blocks, [full(p_shape)] * n, [half] * 2, [full(half)] * 2)
    other = swap(theirs)
    return jnp.where(k == 0, jnp.concatenate([mine, other], 1), jnp.concatenate([other, mine], 1))


def solution(mesh):
    n, n_head = mesh.shape["seq"] // 2, mesh.shape["head"]
    assert n == n_head and n & (n - 1) == 0
    in_specs = (
        P("seq", "head"),
        P("seq", "head"),
        P("seq", None),
        P("seq", None),
        P("head", "seq"),
        P("head", "seq"),
        P("head"),
        P("head"),
        P("head", "seq"),
    )

    def run(*args):
        return body(n, n_head, *args)

    return jax.shard_map(run, mesh=mesh, in_specs=in_specs, out_specs=P("seq", "head"), check_vma=False)
```

```python
import jax
import jax.numpy as jnp
from jax import lax
from jax.experimental import pallas as pl
from jax.experimental.pallas import tpu as pltpu
from jax.sharding import PartitionSpec as P

BOTH = ("seq", "head")
HIGH = lax.Precision.HIGHEST
f32, bf16 = jnp.float32, jnp.bfloat16
EXT = 16
MIB = 1024 * 1024


def call(kernel, scalars, ins, in_specs, outs, out_specs, scratch=(), flops=0, limit=24):
    moved = sum(a.size * a.dtype.itemsize for a in ins) + sum(
        o.size * o.dtype.itemsize for o in outs
    )
    return pl.pallas_call(
        kernel,
        out_shape=outs,
        grid_spec=pltpu.PrefetchScalarGridSpec(
            num_scalar_prefetch=1,
            grid=(1,),
            in_specs=in_specs,
            out_specs=out_specs,
            scratch_shapes=scratch,
        ),
        cost_estimate=pl.CostEstimate(flops=flops, bytes_accessed=moved, transcendentals=0),
        compiler_params=pltpu.CompilerParams(vmem_limit_bytes=limit * MIB),
    )(scalars, *ins)


def full(a):
    return pl.BlockSpec(memory_space=pltpu.VMEM)


def shape(dims, kind):
    return jax.ShapeDtypeStruct(dims, kind)


def nn(a, b, precision=None):
    return jnp.dot(a, b, preferred_element_type=f32, precision=precision)


def nt(a, b, precision=None):
    return lax.dot_general(a, b, (((1,), (1,)), ((), ())), preferred_element_type=f32, precision=precision)


def tn(a, b, precision=None):
    return lax.dot_general(a, b, (((0,), (0,)), ((), ())), preferred_element_type=f32, precision=precision)


def split2(v):
    hi = v.astype(bf16).astype(f32)
    return hi, v - hi


def half_lanes(ref, k):
    n = ref.shape[1] // 2
    return ref[:, pl.ds(pl.multiple_of(k * n, n), n)]


def half_rows(ref, k):
    v = ref[...]
    n = v.shape[0] // 2
    return jnp.where(k == 0, v[:n], v[n:])


def channel_map(heads, wide):
    head = lax.broadcasted_iota(jnp.int32, (heads, wide), 0)
    lane = lax.broadcasted_iota(jnp.int32, (heads, wide), 1)
    size = wide // heads
    return ((lane >= head * size) & (lane < (head + 1) * size)).astype(bf16)


def spread(v, spots):
    hi, lo = split2(v)
    return tn(hi.astype(bf16), spots) + tn(lo.astype(bf16), spots)


def ones_upto(rows):
    i = lax.broadcasted_iota(jnp.int32, (rows, rows), 0)
    j = lax.broadcasted_iota(jnp.int32, (rows, rows), 1)
    return (j <= i), (i <= j)


def state_kernel(s, xo, xr, bo, br, dto, dtr, ldo, ldr, _, msg, first):
    k = s[0]
    rows, wide = xo.shape[0], xo.shape[1] // 2
    _, upper = ones_upto(rows)
    got = []
    for x, b, dt, ld in ((xo, bo, dto, ldo), (xr, br, dtr, ldr)):
        dt, ld = half_rows(dt, k), half_rows(ld, k)
        spots = channel_map(ld.shape[0], wide)
        run = nn(ld, upper.astype(f32), HIGH)
        last = run[:, rows - 1 :]
        tail = jnp.exp(last - run) * dt
        scaled = (half_lanes(x, k).astype(f32) * spread(tail, spots)).astype(bf16)
        state = tn(b[...], scaled)
        decay = spread(jnp.exp(jnp.broadcast_to(last, (last.shape[0], 8))), spots)
        got.append((state, decay))
    (so, do), (sr, dr) = got
    even = k == 0
    s1, s2 = jnp.where(even, so, sr), jnp.where(even, sr, so)
    d2 = jnp.where(even, dr, do)
    n = s1.shape[0]
    msg[:n] = (d2[:1] * s1 + s2).astype(bf16)
    hi, lo = split2(do * dr)
    msg[n:] = jnp.concatenate([hi, lo], 0).astype(bf16)
    first[...] = s1


def unpack(ref):
    n = ref.shape[0] - EXT
    ext = ref[n:].astype(f32)
    return ref[:n].astype(f32), ext[:8] + ext[8:]


def inside_kernel(s, xo, xr, bo, br, co, cr, dto, dtr, ldo, ldr, skip, out):
    k = s[0]
    rows, wide = xo.shape[0], xo.shape[1] // 2
    low, upper = ones_upto(rows)
    count = skip.shape[1] // 2
    gains = jnp.where(k == 0, skip[:, :count], skip[:, count:])
    hi, lo = split2(jnp.broadcast_to(gains, (8, count)))
    spots = channel_map(count, wide)
    gains = nn(hi.astype(bf16), spots) + nn(lo.astype(bf16), spots)
    for turn, (x, b, c, dt, ld) in enumerate(((xo, bo, co, dto, ldo), (xr, br, cr, dtr, ldr))):
        start = pl.multiple_of(jnp.where(k == turn, 0, rows), rows)
        dt, ld = half_rows(dt, k), half_rows(ld, k)
        heads = ld.shape[0]
        size = wide // heads
        run = nn(ld, upper.astype(f32), HIGH)
        down = nt(low.astype(f32), ld, HIGH)
        scores = jnp.where(low, nt(c[...], b[...]), 0.0)
        lane = lax.broadcasted_iota(jnp.int32, (rows, 2 * size), 1)
        for pair in range(heads // 2):
            w = []
            for h in (2 * pair, 2 * pair + 1):
                gap = jnp.minimum(down[:, h : h + 1] - run[h : h + 1, :], 0.0)
                w.append((jnp.exp(gap) * scores * dt[h : h + 1, :]).astype(bf16))
            xp = x[:, pl.ds(pl.multiple_of(k * wide + 2 * pair * size, 2 * size), 2 * size)]
            zero = jnp.zeros_like(xp)
            both = jnp.concatenate([jnp.where(lane < size, xp, zero), jnp.where(lane < size, zero, xp)], 0)
            y = nn(jnp.concatenate(w, 1), both)
            at = slice(2 * pair * size, 2 * (pair + 1) * size)
            out[pl.ds(start, rows), at] = y + gains[:1, at] * xp.astype(f32)


def gate_kernel(s, inside, first, co, cr, ldo, ldr, zo, zr, gain, *rest):
    *states, out, squares = rest
    k = s[0]
    rows, wide = zo.shape[0], zo.shape[1] // 2
    _, upper = ones_upto(rows)
    even = k == 0
    enter, through = jnp.zeros_like(first[...]), None
    for ref in states:
        st, dec = unpack(ref)
        enter = enter + (st if through is None else st * through)
        through = dec[:1] if through is None else through * dec[:1]
    ld1 = jnp.where(even, half_rows(ldo, k), half_rows(ldr, k))
    ld2 = jnp.where(even, half_rows(ldr, k), half_rows(ldo, k))
    c1, c2 = jnp.where(even, co[...], cr[...]), jnp.where(even, cr[...], co[...])
    spots = channel_map(ld1.shape[0], wide)
    ones = jnp.ones((8, wide), bf16)
    for turn, (c, ld) in enumerate(((c1, ld1), (c2, ld2))):
        run = nn(ld, upper.astype(f32), HIGH)
        decays = spread(jnp.exp(run), spots)
        carried = nn(c, enter.astype(bf16)) * decays
        y = inside[turn * rows : (turn + 1) * rows] + carried
        za, zb = (zo, zr) if turn == 0 else (zr, zo)
        zf = jnp.where(even, half_lanes(za, k), half_lanes(zb, k)).astype(f32)
        gated = y * zf / (1.0 + jnp.exp(-zf))
        sq_hi, sq_lo = split2(gated * gated)
        sq = nt(ones, sq_hi.astype(bf16)) + nt(ones, sq_lo.astype(bf16))
        out[turn * rows : (turn + 1) * rows] = (gated * half_lanes(gain, k)).astype(bf16)
        squares[8 * turn : 8 * turn + 8] = sq
        if turn == 0:
            enter = decays[rows - 1 : rows] * enter + first[...]


def project_kernel(s, *refs):
    *g, w, out = refs
    k = s[0]
    parts = len(g) // 2
    rows, depth = g[0].shape
    here = pl.ds(pl.multiple_of(k * depth, depth), depth)
    there = pl.ds(pl.multiple_of((1 - k) * depth, depth), depth)
    for turn in range(parts):
        got = nn(g[turn][...], w[here]) + nn(g[parts + turn][...], w[there])
        out[turn * rows : (turn + 1) * rows] = got.astype(bf16)


def choose_kernel(s, *refs):
    n = (len(refs) - 1) // 2
    ins, outs, sem = refs[:n], refs[n : 2 * n], refs[2 * n]
    for m in range(n):
        for j in range(n):

            @pl.when((s[2] ^ m) == j)
            def _():
                pltpu.make_async_copy(ins[j], outs[m], sem.at[m]).start()

    for m in range(n):
        pltpu.make_async_copy(ins[0], outs[m], sem.at[m]).wait()


def sum_kernel(s, *refs, inner):
    *z, squares, mine, theirs = refs
    k = s[0]
    rows = mine.shape[0]
    i = lax.broadcasted_iota(jnp.int32, (rows, rows), 0)
    j = lax.broadcasted_iota(jnp.int32, (rows, rows), 1)
    done = []
    for turn in range(2):
        row = lax.rsqrt(squares[8 * turn : 8 * turn + 1] / inner + 1e-5)
        col = jnp.sum(jnp.where(i == j, jnp.broadcast_to(row, (rows, rows)), 0.0), axis=1, keepdims=True)
        total = sum(a[turn * rows : (turn + 1) * rows].astype(f32) for a in z)
        done.append((total * col).astype(bf16))
    even = k == 0
    mine[...] = jnp.where(even, done[0], done[1])
    theirs[...] = jnp.where(even, done[1], done[0])


def body(n, n_head, signal, gate_input, state_in, state_out, step_size, log_decay, skip_gain, norm_gain, out_weight):
    rows = signal.shape[0]
    heads = log_decay.shape[0]
    wide = signal.shape[1] // 2
    size = signal.shape[1] // heads
    states = state_in.shape[1]
    cols = out_weight.shape[1]
    place, z = lax.axis_index("seq"), lax.axis_index("head")
    k, chip = place % 2, place // 2
    s = jnp.stack([k, chip, chip ^ z]).astype(jnp.int32)

    def swap(a):
        return lax.ppermute(a, "seq", [(i, i ^ 1) for i in range(2 * n)])

    def across(a, j):
        return lax.ppermute(a, "seq", [(i, i ^ (2 * j)) for i in range(2 * n)])

    x2, b2 = swap(signal), swap(state_in)
    dt2, ld2 = swap(step_size), swap(log_decay)
    z2, c2 = swap(gate_input), swap(state_out)
    skip = skip_gain.reshape(1, heads)
    gain = norm_gain.reshape(1, 2 * wide)

    any_spec = pl.BlockSpec(memory_space=pl.ANY)
    ins = (signal, x2, state_in, b2, step_size, dt2, log_decay, ld2, c2)
    specs = [full(signal)] * 2 + [full(state_in)] * 2 + [full(step_size)] * 4 + [any_spec]
    msg_shape = shape((states + EXT, wide), bf16)
    first_shape = shape((states, wide), f32)
    msg, first = call(state_kernel, s, ins, specs, [msg_shape, first_shape], [full(msg_shape), full(first_shape)])
    got = [
        lax.ppermute(msg, "seq", [(i, i + 2 * j) for i in range(2 * (n - j))]) for j in range(1, n)
    ]
    ins = (signal, x2, state_in, b2, state_out, c2, step_size, dt2, log_decay, ld2, skip)
    specs = [full(signal)] * 2 + [full(state_in)] * 4 + [full(step_size)] * 4 + [full(skip)]
    inside_shape = shape((2 * rows, wide), f32)
    (inside,) = call(inside_kernel, s, ins, specs, [inside_shape], [full(inside_shape)])

    ins = (inside, first, state_out, c2, log_decay, ld2, gate_input, z2, gain, *got)
    specs = [full(inside), full(first), full(state_out), full(c2), full(log_decay), full(ld2)]
    specs += [full(gate_input)] * 2 + [full(gain)] + [full(m) for m in got]
    g_shape, sq_shape = shape((2 * rows, wide), bf16), shape((16, rows), f32)
    g, squares = call(gate_kernel, s, ins, specs, [g_shape, sq_shape], [full(g_shape), full(sq_shape)])

    p_shape = shape((2 * rows, cols), bf16)

    def project(*g):
        ins = (*g, *[swap(a) for a in g], out_weight)
        return call(project_kernel, s, ins, [full(a) for a in ins], [p_shape], [full(p_shape)])[0]

    if n == 4:
        gx, gy = across(g, 1), across(g, 2)
        squares = squares + swap(squares)
        for bit in range(2):
            squares = squares + lax.ppermute(squares, "head", [(i, i ^ (1 << bit)) for i in range(n)])
        own = project(g)
        gx, gy, own, squares = lax.optimization_barrier((gx, gy, own, squares))
        fx, fy = across(gx[:rows], 2), across(gy[rows:], 1)
        px, py = project(gx), project(gy)
        fx, fy, px, py = lax.optimization_barrier((fx, fy, px, py))
        blocks = [own, px, py, project(fx, fy)]
    else:
        squares = squares + swap(squares)
        for bit in range(n.bit_length() - 1):
            squares = squares + lax.ppermute(squares, "head", [(i, i ^ (1 << bit)) for i in range(n)])
        blocks = [project(g)] + [project(across(g, j)) for j in range(1, n)]
    blocks = [blocks[0]] + [across(blocks[j], j) for j in range(1, n)]

    blocks = call(
        choose_kernel, s, blocks, [any_spec] * n, [p_shape] * n, [any_spec] * n,
        scratch=[pltpu.SemaphoreType.DMA((n,))],
    )
    blocks = [blocks[0]] + [
        lax.ppermute(blocks[m], "head", [(i, i ^ m) for i in range(n)]) for m in range(1, n)
    ]
    half = shape((rows, cols), bf16)

    def add(*refs):
        sum_kernel(*refs, inner=2 * wide * n_head)

    ins = (*blocks, squares)
    mine, theirs = call(add, s, ins, [full(a) for a in ins], [half] * 2, [full(half)] * 2)
    other = swap(theirs)
    return jnp.where(k == 0, jnp.concatenate([mine, other], 1), jnp.concatenate([other, mine], 1))


def solution(mesh):
    n, n_head = mesh.shape["seq"] // 2, mesh.shape["head"]
    assert n == n_head and n & (n - 1) == 0
    in_specs = (
        P("seq", "head"),
        P("seq", "head"),
        P("seq", None),
        P("seq", None),
        P("head", "seq"),
        P("head", "seq"),
        P("head"),
        P("head"),
        P("head", "seq"),
    )

    def run(*args):
        return body(n, n_head, *args)

    return jax.shard_map(run, mesh=mesh, in_specs=in_specs, out_specs=P("seq", "head"), check_vma=False)
```

```python
import jax
import jax.numpy as jnp
from jax import lax
from jax.experimental import pallas as pl
from jax.experimental.pallas import tpu as pltpu
from jax.sharding import PartitionSpec as P

BOTH = ("seq", "head")
HIGH = lax.Precision.HIGHEST
f32, bf16 = jnp.float32, jnp.bfloat16
EXT = 16
LANES = 128
MIB = 1024 * 1024


def call(kernel, scalars, ins, in_specs, outs, out_specs, scratch=(), flops=0, limit=24):
    moved = sum(a.size * a.dtype.itemsize for a in ins) + sum(
        o.size * o.dtype.itemsize for o in outs
    )
    return pl.pallas_call(
        kernel,
        out_shape=outs,
        grid_spec=pltpu.PrefetchScalarGridSpec(
            num_scalar_prefetch=1,
            grid=(1,),
            in_specs=in_specs,
            out_specs=out_specs,
            scratch_shapes=scratch,
        ),
        cost_estimate=pl.CostEstimate(flops=flops, bytes_accessed=moved, transcendentals=0),
        compiler_params=pltpu.CompilerParams(vmem_limit_bytes=limit * MIB),
    )(scalars, *ins)


def full(a):
    return pl.BlockSpec(memory_space=pltpu.VMEM)


def shape(dims, kind):
    return jax.ShapeDtypeStruct(dims, kind)


def nn(a, b, precision=None):
    return jnp.dot(a, b, preferred_element_type=f32, precision=precision)


def nt(a, b, precision=None):
    return lax.dot_general(a, b, (((1,), (1,)), ((), ())), preferred_element_type=f32, precision=precision)


def tn(a, b, precision=None):
    return lax.dot_general(a, b, (((0,), (0,)), ((), ())), preferred_element_type=f32, precision=precision)


def split2(v):
    hi = v.astype(bf16).astype(f32)
    return hi, v - hi


def half_lanes(ref, k):
    n = ref.shape[1] // 2
    return ref[:, pl.ds(pl.multiple_of(k * n, n), n)]


def half_rows(ref, k):
    v = ref[...]
    n = v.shape[0] // 4
    return tuple(jnp.where(k == 0, v[i : i + n], v[i + n : i + 2 * n]) for i in (0, 2 * n))


def channel_map(heads, wide):
    head = lax.broadcasted_iota(jnp.int32, (heads, wide), 0)
    lane = lax.broadcasted_iota(jnp.int32, (heads, wide), 1)
    size = wide // heads
    return ((lane >= head * size) & (lane < (head + 1) * size)).astype(bf16)


def spread(v, spots):
    hi, lo = split2(v)
    return tn(hi.astype(bf16), spots) + tn(lo.astype(bf16), spots)


def ones_upto(rows):
    i = lax.broadcasted_iota(jnp.int32, (rows, rows), 0)
    j = lax.broadcasted_iota(jnp.int32, (rows, rows), 1)
    return (j <= i), (i <= j)


def state_kernel(s, xo, xr, bo, br, ro, rr, msg, first):
    k = s[0]
    rows, wide = xo.shape
    half = pl.ds(pl.multiple_of(k * wide, wide), wide)
    _, upper = ones_upto(rows)
    got = []
    for x, bc, rates in ((xo[...], bo, ro), (xr[:, half], br, rr)):
        dt, ld = half_rows(rates, k)
        spots = channel_map(ld.shape[0], wide)
        run = nn(ld, upper.astype(f32), HIGH)
        last = run[:, rows - 1 :]
        tail = jnp.exp(last - run) * dt
        scaled = (x.astype(f32) * spread(tail, spots)).astype(bf16)
        state = tn(bc[:, : bc.shape[1] // 2], scaled)
        decay = spread(jnp.exp(jnp.broadcast_to(last, (last.shape[0], 8))), spots)
        got.append((state, decay))
    (so, do), (sr, dr) = got
    even = k == 0
    s1, s2 = jnp.where(even, so, sr), jnp.where(even, sr, so)
    d2 = jnp.where(even, dr, do)
    n = s1.shape[0]
    flat(msg, (d2[:1] * s1 + s2).astype(bf16))
    msg[wide * n // LANES :] = pair(jnp.concatenate([(do * dr)[:1, i : i + LANES] for i in range(0, wide, LANES)], 0))
    first[...] = s1


def flat(ref, value):
    rows = value.shape[0]
    for i in range(value.shape[1] // LANES):
        ref[i * rows : (i + 1) * rows] = value[:, i * LANES : (i + 1) * LANES]


def pair(v):
    if v.shape[0] < 8:
        v = jnp.concatenate([v, jnp.zeros((8 - v.shape[0], v.shape[1]), f32)], 0)
    hi, lo = split2(v)
    return jnp.concatenate([hi, lo], 0).astype(bf16)


def unpair(v):
    v = v.astype(f32)
    return v[:8] + v[8:]


def unpack(ref, n, wide):
    count = wide // LANES
    state = jnp.concatenate([ref[i * n : (i + 1) * n].astype(f32) for i in range(count)], 1)
    ext = unpair(ref[count * n :])
    return state, jnp.concatenate([ext[i : i + 1] for i in range(count)], 1)


def inside_kernel(s, xo, xr, bo, br, ro, rr, zo, zr, skip, out, decays, gates):
    k = s[0]
    rows, wide = xo.shape
    half = pl.ds(pl.multiple_of(k * wide, wide), wide)
    low, upper = ones_upto(rows)
    count = skip.shape[1] // 2
    gains = jnp.where(k == 0, skip[:, :count], skip[:, count:])
    hi, lo = split2(jnp.broadcast_to(gains, (8, count)))
    spots = channel_map(count, wide)
    gains = nn(hi.astype(bf16), spots) + nn(lo.astype(bf16), spots)
    for turn, (bc, rates, z) in enumerate(((bo, ro, zo), (br, rr, zr))):
        start = turn * rows
        dt, ld = half_rows(rates, k)
        heads = ld.shape[0]
        size = wide // heads
        run = nn(ld, upper.astype(f32), HIGH)
        down = nt(low.astype(f32), ld, HIGH)
        decays[start : start + rows] = spread(jnp.exp(run), spots)
        zf = z[:, half].astype(f32)
        gates[start : start + rows] = zf / (1.0 + jnp.exp(-zf))
        states = bc.shape[1] // 2
        scores = jnp.where(low, nt(bc[:, states:], bc[:, :states]), 0.0)
        lane = lax.broadcasted_iota(jnp.int32, (rows, 2 * size), 1)
        for pair in range(heads // 2):
            w = []
            for h in (2 * pair, 2 * pair + 1):
                gap = jnp.minimum(down[:, h : h + 1] - run[h : h + 1, :], 0.0)
                w.append((jnp.exp(gap) * scores * dt[h : h + 1, :]).astype(bf16))
            at = slice(2 * pair * size, 2 * (pair + 1) * size)
            if turn == 0:
                xp = xo[:, at]
            else:
                xp = xr[:, pl.ds(pl.multiple_of(k * wide + 2 * pair * size, 2 * size), 2 * size)]
            zero = jnp.zeros_like(xp)
            both = jnp.concatenate([jnp.where(lane < size, xp, zero), jnp.where(lane < size, zero, xp)], 0)
            y = nn(jnp.concatenate(w, 1), both)
            out[start : start + rows, at] = y + gains[:1, at] * xp.astype(f32)


def gate_kernel(s, inside, decays, gates, first, bo, br, gain, _, *rest):
    *states, mine, theirs, sq_mine, sq_theirs = rest
    k = s[0]
    rows, wide = mine.shape
    even = k == 0
    enter, through = None, None
    for ref in states:
        st, dec = unpack(ref, first.shape[0], wide)
        enter = st if enter is None else enter + st * through
        through = dec if through is None else through * dec
    whole = jnp.where(even, decays[rows - 1 : rows], decays[2 * rows - 1 : 2 * rows])
    second = whole * enter + first[...]
    ones = jnp.ones((8, wide), bf16)
    for turn, (bc, out, sq) in enumerate(((bo, mine, sq_mine), (br, theirs, sq_theirs))):
        at = slice(turn * rows, (turn + 1) * rows)
        e = jnp.where(even, enter, second) if turn == 0 else jnp.where(even, second, enter)
        y = inside[at] + nn(bc[:, bc.shape[1] // 2 :], e.astype(bf16)) * decays[at]
        gated = y * gates[at]
        hi, lo = split2(gated * gated)
        sq[...] = nt(ones, hi.astype(bf16)) + nt(ones, lo.astype(bf16))
        out[...] = (gated * half_lanes(gain, k)).astype(bf16)


def project_kernel(s, *refs, count, extra):
    u, v = refs[:count], refs[count : 2 * count]
    w_own, w_other = refs[2 * count : 2 * count + 2]
    outs = refs[2 * count + 2 + extra :]
    k = s[0]
    rows, depth = u[0].shape
    cols = w_own.shape[1]
    here = pl.ds(pl.multiple_of(k * depth, depth), depth)
    there = pl.ds(pl.multiple_of((1 - k) * depth, depth), depth)
    uu = jnp.concatenate([a[...] for a in u], 0)
    vv = jnp.concatenate([a[...] for a in v], 0)
    for w, place in ((w_own, k), (w_other, 1 - k)):
        got = (nn(uu, w[here]) + nn(vv, w[there])).astype(bf16)
        groups = cols // LANES
        for i, out in enumerate(outs):
            for j in range(groups):
                at = pl.ds(pl.multiple_of((place * groups + j) * rows, rows), rows)
                out[at] = got[i * rows : (i + 1) * rows, j * LANES : (j + 1) * LANES]


def pick(s, m, blocks, do):
    for j, block in enumerate(blocks):

        @pl.when((s[1] ^ m) == j)
        def _():
            do(block)


def choose_kernel(s, *refs, steps):
    count = len(refs) - 1 - len(steps)
    blocks, squares, outs = refs[:count], refs[count], refs[count + 1 :]
    n = blocks[0].shape[0]
    for m, out in zip(steps, outs):

        def copy(block, out=out):
            out[:n] = block[...]

        pick(s, m, blocks, copy)
        out[n:] = pair(squares[...])


def halves_kernel(s, *refs):
    *blocks, squares, top, low, other = refs
    n = low.shape[0]

    def cut(block):
        top[:n] = block[:n]
        low[...] = block[n:]

    def copy(block):
        other[: 2 * n] = block[...]

    pick(s, 3, blocks, cut)
    pick(s, 1, blocks, copy)
    ext = pair(squares[...])
    top[n:] = ext
    other[2 * n :] = ext


def join_kernel(s, *refs, base):
    *blocks, squares, got, out = refs
    n = blocks[0].shape[0] // 2

    def add(block):
        out[:n] = (block[base * n : (base + 1) * n].astype(f32) + got[:n].astype(f32)).astype(bf16)

    pick(s, 2, blocks, add)
    if base == 0:
        out[n:] = pair(squares[...] + unpair(got[n:]))


def sum_kernel(s, *refs, inner, count):
    blocks, (squares, *got, out) = refs[:count], refs[count:]
    rows = out.shape[0]
    groups = out.shape[1] // LANES
    size = groups * rows
    i = lax.broadcasted_iota(jnp.int32, (rows, rows), 0)
    j = lax.broadcasted_iota(jnp.int32, (rows, rows), 1)
    total = squares[...] + sum(unpair(a[a.shape[0] - EXT :]) for a in got if a.shape[0] % size % (size // 2) == EXT)
    row = lax.rsqrt(total[:1] / inner + 1e-5)
    col = jnp.sum(jnp.where(i == j, jnp.broadcast_to(row, (rows, rows)), 0.0), axis=1, keepdims=True)

    def finish(block):
        for g in range(groups):
            v = block[g * rows : (g + 1) * rows].astype(f32)
            at = 0
            for a in got:
                span = a.shape[0] // rows
                if span == groups:
                    v += a[g * rows : (g + 1) * rows].astype(f32)
                else:
                    if at <= g < at + span:
                        v += a[(g - at) * rows : (g - at + 1) * rows].astype(f32)
                    at += span
            out[:, g * LANES : (g + 1) * LANES] = (v * col).astype(bf16)

    pick(s, 0, blocks, finish)


def body(n, n_head, signal, gate_input, state_in, state_out, step_size, log_decay, skip_gain, norm_gain, out_weight):
    rows = signal.shape[0]
    heads = log_decay.shape[0]
    wide = signal.shape[1] // 2
    states = state_in.shape[1]
    cols = out_weight.shape[1]
    place, z = lax.axis_index("seq"), lax.axis_index("head")
    k, chip = place % 2, place // 2
    s = jnp.stack([k, chip ^ z]).astype(jnp.int32)
    any_spec = pl.BlockSpec(memory_space=pl.ANY)

    def swap(a):
        return lax.ppermute(a, "seq", [(i, i ^ 1) for i in range(2 * n)])

    def across(a, j):
        return lax.ppermute(a, "seq", [(i, i ^ (2 * j)) for i in range(2 * n)])

    def along(a, m):
        return lax.ppermute(a, "head", [(i, i ^ m) for i in range(n)])

    x2 = swap(signal)
    rates1 = jnp.concatenate([step_size, log_decay], 0)
    bc1 = jnp.concatenate([state_in, state_out], 1)
    rates2, bc2 = swap(rates1), swap(bc1)
    z2 = swap(gate_input)
    x1 = lax.dynamic_slice_in_dim(signal, k * wide, wide, 1)
    skip = skip_gain.reshape(1, heads)
    gain = norm_gain.reshape(1, 2 * wide)

    ins = (x1, x2, bc1, bc2, rates1, rates2)
    outs = [shape((states * wide // LANES + EXT, LANES), bf16), shape((states, wide), f32)]
    msg, first = call(state_kernel, s, ins, [full(a) for a in ins], outs, [full(a) for a in outs])
    w2 = swap(lax.optimization_barrier((out_weight, msg))[0])
    got = [
        lax.ppermute(msg, "seq", [(i, i + 2 * j) for i in range(2 * (n - j))]) for j in range(1, n)
    ]
    ins = (x1, x2, bc1, bc2, rates1, rates2, gate_input, z2, skip)
    big = shape((2 * rows, wide), f32)
    inside, decays, gates = call(
        inside_kernel, s, ins, [full(a) for a in ins], [big] * 3, [full(big)] * 3
    )
    ins = (inside, decays, gates, first, bc1, bc2, gain, w2, *got)
    specs = [full(a) for a in ins[:7]] + [any_spec] + [full(a) for a in got]
    outs = [shape((rows, wide), bf16)] * 2 + [shape((8, rows), f32)] * 2
    u, v, sq_mine, sq_theirs = call(gate_kernel, s, ins, specs, outs, [full(a) for a in outs])
    squares = sq_mine + swap(sq_theirs)

    size = 2 * cols // LANES * rows
    p_shape = shape((size, LANES), bf16)

    def project(u, v, after=()):
        ins = (*u, *v, out_weight, w2, *after)
        specs = [full(a) for a in ins[: len(ins) - len(after)]] + [any_spec] * len(after)

        def kernel(*refs):
            project_kernel(*refs, count=len(u), extra=len(after))

        return call(kernel, s, ins, specs, [p_shape] * len(u), [full(p_shape)] * len(u))

    if n == 4:
        ux, vy = across(u, 1), across(v, 2)
        vx, uy = across(v, 1), across(u, 2)
        (own,) = project([u], [swap(v)])
        ux, vy, own = lax.optimization_barrier((ux, vy, own))
        ud, vd = lax.optimization_barrier((across(ux, 2), across(vy, 1)))
        near = project([ux, uy], [swap(vx), swap(vy)], after=[own])
        blocks = [own] + [across(near[0], 1), across(near[1], 2)]
        (far,) = project([ud], [swap(vd)], after=blocks[1:])
        blocks.append(across(far, 3))
    else:
        blocks = list(project([u], [swap(v)]))
        for j in range(1, n):
            (p,) = project([across(u, j)], [swap(across(v, j))])
            blocks.append(across(p, j))
    message = shape((size + EXT, LANES), bf16)

    def send(kernel, ins, outs, **kw):
        def run(*refs):
            kernel(*refs, **kw)

        return call(run, s, ins, [full(a) for a in ins], outs, [full(a) for a in outs])

    if n == 4:
        tall, short = shape((size // 2 + EXT, LANES), bf16), shape((size // 2, LANES), bf16)
        top, low, other = send(halves_kernel, (*blocks, squares), [tall, short, message])
        top, low, other = along(top, 1), along(low, 1), along(other, 1)
        (top,) = send(join_kernel, (*blocks, squares, top), [tall], base=0)
        (low,) = send(join_kernel, (*blocks, squares, low), [short], base=1)
        got = (other, along(top, 2), along(low, 2))
    else:
        steps = range(1, n)
        got = send(choose_kernel, (*blocks, squares), [message] * (n - 1), steps=steps)
        got = [along(a, m) for a, m in zip(got, steps)]
    return send(
        sum_kernel, (*blocks, squares, *got), [shape((rows, 2 * cols), bf16)],
        inner=2 * wide * n_head, count=n,
    )[0]


def solution(mesh):
    n, n_head = mesh.shape["seq"] // 2, mesh.shape["head"]
    assert n == n_head and n & (n - 1) == 0
    in_specs = (
        P("seq", "head"),
        P("seq", "head"),
        P("seq", None),
        P("seq", None),
        P("head", "seq"),
        P("head", "seq"),
        P("head"),
        P("head"),
        P("head", "seq"),
    )

    def run(*args):
        return body(n, n_head, *args)

    return jax.shard_map(run, mesh=mesh, in_specs=in_specs, out_specs=P("seq", "head"), check_vma=False)
```

```python
import jax
import jax.numpy as jnp
from jax import lax
from jax.experimental import pallas as pl
from jax.experimental.pallas import tpu as pltpu
from jax.sharding import PartitionSpec as P

BOTH = ("seq", "head")
HIGH = lax.Precision.HIGHEST
f32, bf16 = jnp.float32, jnp.bfloat16
EXT = 16
LANES = 128
MIB = 1024 * 1024


def call(kernel, scalars, ins, in_specs, outs, out_specs, scratch=(), flops=0, limit=24):
    moved = sum(a.size * a.dtype.itemsize for a in ins) + sum(
        o.size * o.dtype.itemsize for o in outs
    )
    return pl.pallas_call(
        kernel,
        out_shape=outs,
        grid_spec=pltpu.PrefetchScalarGridSpec(
            num_scalar_prefetch=1,
            grid=(1,),
            in_specs=in_specs,
            out_specs=out_specs,
            scratch_shapes=scratch,
        ),
        cost_estimate=pl.CostEstimate(flops=flops, bytes_accessed=moved, transcendentals=0),
        compiler_params=pltpu.CompilerParams(vmem_limit_bytes=limit * MIB),
    )(scalars, *ins)


def full(a):
    return pl.BlockSpec(memory_space=pltpu.VMEM)


def shape(dims, kind):
    return jax.ShapeDtypeStruct(dims, kind)


def nn(a, b, precision=None):
    return jnp.dot(a, b, preferred_element_type=f32, precision=precision)


def nt(a, b, precision=None):
    return lax.dot_general(a, b, (((1,), (1,)), ((), ())), preferred_element_type=f32, precision=precision)


def tn(a, b, precision=None):
    return lax.dot_general(a, b, (((0,), (0,)), ((), ())), preferred_element_type=f32, precision=precision)


def split2(v):
    hi = v.astype(bf16).astype(f32)
    return hi, v - hi


def half_lanes(ref, k):
    n = ref.shape[1] // 2
    return ref[:, pl.ds(pl.multiple_of(k * n, n), n)]


def half_rows(ref, k):
    v = ref[...]
    n = v.shape[0] // 4
    return tuple(jnp.where(k == 0, v[i : i + n], v[i + n : i + 2 * n]) for i in (0, 2 * n))


def channel_map(heads, wide):
    head = lax.broadcasted_iota(jnp.int32, (heads, wide), 0)
    lane = lax.broadcasted_iota(jnp.int32, (heads, wide), 1)
    size = wide // heads
    return ((lane >= head * size) & (lane < (head + 1) * size)).astype(bf16)


def spread(v, spots):
    hi, lo = split2(v)
    return tn(hi.astype(bf16), spots) + tn(lo.astype(bf16), spots)


def ones_upto(rows):
    i = lax.broadcasted_iota(jnp.int32, (rows, rows), 0)
    j = lax.broadcasted_iota(jnp.int32, (rows, rows), 1)
    return (j <= i), (i <= j)


def state_kernel(s, xo, xr, bo, br, ro, rr, msg, first):
    k = s[0]
    rows, wide = xo.shape
    half = pl.ds(pl.multiple_of(k * wide, wide), wide)
    _, upper = ones_upto(rows)
    got = []
    for x, bc, rates in ((xo[...], bo, ro), (xr[:, half], br, rr)):
        dt, ld = half_rows(rates, k)
        spots = channel_map(ld.shape[0], wide)
        run = nn(ld, upper.astype(f32), HIGH)
        last = run[:, rows - 1 :]
        tail = jnp.exp(last - run) * dt
        scaled = (x.astype(f32) * spread(tail, spots)).astype(bf16)
        state = tn(bc[:, : bc.shape[1] // 2], scaled)
        decay = spread(jnp.exp(jnp.broadcast_to(last, (last.shape[0], 8))), spots)
        got.append((state, decay))
    (so, do), (sr, dr) = got
    even = k == 0
    s1, s2 = jnp.where(even, so, sr), jnp.where(even, sr, so)
    d2 = jnp.where(even, dr, do)
    n = s1.shape[0]
    flat(msg, (d2[:1] * s1 + s2).astype(bf16))
    msg[wide * n // LANES :] = pair(jnp.concatenate([(do * dr)[:1, i : i + LANES] for i in range(0, wide, LANES)], 0))
    first[...] = s1


def flat(ref, value):
    rows = value.shape[0]
    for i in range(value.shape[1] // LANES):
        ref[i * rows : (i + 1) * rows] = value[:, i * LANES : (i + 1) * LANES]


def pair(v):
    if v.shape[0] < 8:
        v = jnp.concatenate([v, jnp.zeros((8 - v.shape[0], v.shape[1]), f32)], 0)
    hi, lo = split2(v)
    return jnp.concatenate([hi, lo], 0).astype(bf16)


def unpair(v):
    v = v.astype(f32)
    return v[:8] + v[8:]


def unpack(ref, n, wide):
    count = wide // LANES
    state = jnp.concatenate([ref[i * n : (i + 1) * n].astype(f32) for i in range(count)], 1)
    ext = unpair(ref[count * n :])
    return state, jnp.concatenate([ext[i : i + 1] for i in range(count)], 1)


def inside_kernel(s, xo, xr, bo, br, ro, rr, zo, zr, skip, out, decays, gates):
    k = s[0]
    rows, wide = xo.shape
    half = pl.ds(pl.multiple_of(k * wide, wide), wide)
    low, upper = ones_upto(rows)
    count = skip.shape[1] // 2
    gains = jnp.where(k == 0, skip[:, :count], skip[:, count:])
    hi, lo = split2(jnp.broadcast_to(gains, (8, count)))
    spots = channel_map(count, wide)
    gains = nn(hi.astype(bf16), spots) + nn(lo.astype(bf16), spots)
    for turn, (bc, rates, z) in enumerate(((bo, ro, zo), (br, rr, zr))):
        start = turn * rows
        dt, ld = half_rows(rates, k)
        heads = ld.shape[0]
        size = wide // heads
        run = nn(ld, upper.astype(f32), HIGH)
        down = nt(low.astype(f32), ld, HIGH)
        decays[start : start + rows] = spread(jnp.exp(run), spots)
        zf = z[:, half].astype(f32)
        gates[start : start + rows] = zf / (1.0 + jnp.exp(-zf))
        states = bc.shape[1] // 2
        scores = jnp.where(low, nt(bc[:, states:], bc[:, :states]), 0.0)
        lane = lax.broadcasted_iota(jnp.int32, (rows, 2 * size), 1)
        for pair in range(heads // 2):
            w = []
            for h in (2 * pair, 2 * pair + 1):
                gap = jnp.minimum(down[:, h : h + 1] - run[h : h + 1, :], 0.0)
                w.append((jnp.exp(gap) * scores * dt[h : h + 1, :]).astype(bf16))
            at = slice(2 * pair * size, 2 * (pair + 1) * size)
            if turn == 0:
                xp = xo[:, at]
            else:
                xp = xr[:, pl.ds(pl.multiple_of(k * wide + 2 * pair * size, 2 * size), 2 * size)]
            zero = jnp.zeros_like(xp)
            both = jnp.concatenate([jnp.where(lane < size, xp, zero), jnp.where(lane < size, zero, xp)], 0)
            y = nn(jnp.concatenate(w, 1), both)
            out[start : start + rows, at] = y + gains[:1, at] * xp.astype(f32)


def gate_kernel(s, inside, decays, gates, first, bo, br, gain, _, *rest):
    *states, mine, theirs, sq_mine, sq_theirs = rest
    k = s[0]
    rows, wide = mine.shape
    even = k == 0
    enter, through = None, None
    for j, ref in enumerate(states):
        st, dec = unpack(ref, first.shape[0], wide)
        st = jnp.where(s[2] > j, st, 0.0)
        enter = st if enter is None else enter + st * through
        through = dec if through is None else through * dec
    whole = jnp.where(even, decays[rows - 1 : rows], decays[2 * rows - 1 : 2 * rows])
    second = whole * enter + first[...]
    ones = jnp.ones((8, wide), bf16)
    for turn, (bc, out, sq) in enumerate(((bo, mine, sq_mine), (br, theirs, sq_theirs))):
        at = slice(turn * rows, (turn + 1) * rows)
        e = jnp.where(even, enter, second) if turn == 0 else jnp.where(even, second, enter)
        y = inside[at] + nn(bc[:, bc.shape[1] // 2 :], e.astype(bf16)) * decays[at]
        gated = y * gates[at]
        hi, lo = split2(gated * gated)
        sq[...] = nt(ones, hi.astype(bf16)) + nt(ones, lo.astype(bf16))
        out[...] = (gated * half_lanes(gain, k)).astype(bf16)


def project_kernel(s, *refs, count, extra):
    u, v = refs[:count], refs[count : 2 * count]
    w_own, w_other = refs[2 * count : 2 * count + 2]
    outs = refs[2 * count + 2 + extra :]
    k = s[0]
    rows, depth = u[0].shape
    cols = w_own.shape[1]
    groups = cols // LANES
    here = pl.ds(pl.multiple_of(k * depth, depth), depth)
    there = pl.ds(pl.multiple_of((1 - k) * depth, depth), depth)
    uu = jnp.concatenate([a[...] for a in u], 0)
    vv = jnp.concatenate([a[...] for a in v], 0)
    for w, place in ((w_own, k), (w_other, 1 - k)):
        got = (nn(uu, w[here]) + nn(vv, w[there])).astype(bf16)
        for i, out in enumerate(outs):
            for j in range(groups):
                at = pl.ds(pl.multiple_of((place * groups + j) * rows, rows), rows)
                out[at] = got[i * rows : (i + 1) * rows, j * LANES : (j + 1) * LANES]


def pick(s, m, blocks, do):
    for j, block in enumerate(blocks):

        @pl.when((s[1] ^ m) == j)
        def _():
            do(block)


def choose_kernel(s, *refs, steps):
    blocks, squares, outs = refs[:-1 - len(steps)], refs[-1 - len(steps)], refs[-len(steps) :]
    n = blocks[0].shape[0]
    for m, out in zip(steps, outs):

        def copy(block, out=out):
            out[:n] = block[...]

        pick(s, m, blocks, copy)
        out[n:] = pair(squares[...])


def give_kernel(s, even, odd, *refs):
    out = refs[-1]
    n = even.shape[0]
    out[:n] = jnp.where((s[1] & 1) == 0, even[...], odd[...])
    if out.shape[0] > n:
        out[n:] = pair(refs[0][...])


def join_kernel(s, even, odd, got, squares, ext, *rest):
    out = rest[-1]
    n = even.shape[0]
    kept = jnp.where((s[1] & 1) == 0, even[...], odd[...])
    out[:n] = (kept.astype(f32) + got[:n].astype(f32)).astype(bf16)
    out[n:] = pair(squares[...] + unpair(ext[n:]))


def row_scale(total, inner, rows):
    i = lax.broadcasted_iota(jnp.int32, (rows, rows), 0)
    j = lax.broadcasted_iota(jnp.int32, (rows, rows), 1)
    row = lax.rsqrt(total[:1] / inner + 1e-5)
    return jnp.sum(jnp.where(i == j, jnp.broadcast_to(row, (rows, rows)), 0.0), axis=1, keepdims=True)


def sum_kernel(s, *refs, inner):
    count = len(refs) // 2 - 1
    blocks, squares, got, out = refs[: count + 1], refs[count + 1], refs[count + 2 : -1], refs[-1]
    rows = out.shape[0]
    n = blocks[0].shape[0]
    col = row_scale(squares[...] + sum(unpair(a[n:]) for a in got), inner, rows)

    def finish(block):
        for g in range(n // rows):
            at = slice(g * rows, (g + 1) * rows)
            v = block[at].astype(f32) + sum(a[at].astype(f32) for a in got)
            out[:, g * LANES : (g + 1) * LANES] = (v * col).astype(bf16)

    pick(s, 0, blocks, finish)


def last_kernel(s, own, x, y, far, got1, got2, sum1, sum2, squares, out, *, inner):
    rows = out.shape[0]
    n = own.shape[0]
    base = squares[...] + unpair(got1[n:])

    def finish(block, got, other):
        col = row_scale(base + unpair(other[n:]), inner, rows)
        for g in range(n // rows):
            at = slice(g * rows, (g + 1) * rows)
            v = block[at].astype(f32) + got[at].astype(f32) + other[at].astype(f32)
            out[:, g * LANES : (g + 1) * LANES] = (v * col).astype(bf16)

    for turn, args in enumerate(((own, got2, sum2), (x, got1, sum1), (y, got1, sum1), (far, got2, sum2))):

        @pl.when(s[1] == turn)
        def _():
            finish(*args)


def body(n, n_head, signal, gate_input, state_in, state_out, step_size, log_decay, skip_gain, norm_gain, out_weight):
    rows = signal.shape[0]
    heads = log_decay.shape[0]
    wide = signal.shape[1] // 2
    states = state_in.shape[1]
    cols = out_weight.shape[1]
    place, z = lax.axis_index("seq"), lax.axis_index("head")
    k, chip = place % 2, place // 2
    s = jnp.stack([k, chip ^ z, chip]).astype(jnp.int32)
    any_spec = pl.BlockSpec(memory_space=pl.ANY)

    def swap(a):
        return lax.ppermute(a, "seq", [(i, i ^ 1) for i in range(2 * n)])

    def across(a, j):
        return lax.ppermute(a, "seq", [(i, i ^ (2 * j)) for i in range(2 * n)])

    def along(a, m):
        return lax.ppermute(a, "head", [(i, i ^ m) for i in range(n)])

    x2 = swap(signal)
    rates1 = jnp.pad(step_size, ((0, heads), (0, 0))) + jnp.pad(log_decay, ((heads, 0), (0, 0)))
    states = state_in.shape[1]
    bc1 = jnp.pad(state_in, ((0, 0), (0, states))) + jnp.pad(state_out, ((0, 0), (states, 0)))
    rates2, bc2 = swap(rates1), swap(bc1)
    z2 = swap(gate_input)
    x1 = lax.dynamic_slice_in_dim(signal, k * wide, wide, 1)
    skip = skip_gain.reshape(1, heads)
    gain = norm_gain.reshape(1, 2 * wide)

    ins = (x1, x2, bc1, bc2, rates1, rates2)
    outs = [shape((states * wide // LANES + EXT, LANES), bf16), shape((states, wide), f32)]
    msg, first = call(state_kernel, s, ins, [full(a) for a in ins], outs, [full(a) for a in outs])
    w2 = swap(lax.optimization_barrier((out_weight, msg))[0])
    got = [
        lax.ppermute(msg, "seq", [(i, (i + 2 * j) % (2 * n)) for i in range(2 * n)]) for j in range(1, n)
    ]
    ins = (x1, x2, bc1, bc2, rates1, rates2, gate_input, z2, skip)
    big = shape((2 * rows, wide), f32)
    inside, decays, gates = call(
        inside_kernel, s, ins, [full(a) for a in ins], [big] * 3, [full(big)] * 3
    )
    ins = (inside, decays, gates, first, bc1, bc2, gain, w2, *got)
    specs = [full(a) for a in ins[:7]] + [any_spec] + [full(a) for a in got]
    outs = [shape((rows, wide), bf16)] * 2 + [shape((8, rows), f32)] * 2
    u, v, sq_mine, sq_theirs = call(gate_kernel, s, ins, specs, outs, [full(a) for a in outs])
    squares = sq_mine + swap(sq_theirs)

    size = 2 * cols // LANES * rows
    p_shape = shape((size, LANES), bf16)

    def project(u, v, after=()):
        ins = (*u, *v, out_weight, w2, *after)
        specs = [full(a) for a in ins[: len(ins) - len(after)]] + [any_spec] * len(after)

        def kernel(*refs):
            project_kernel(*refs, count=len(u), extra=len(after))

        return call(kernel, s, ins, specs, [p_shape] * len(u), [full(p_shape)] * len(u))

    if n == 4:
        ux, vy = across(u, 1), across(v, 2)
        vx, uy = across(v, 1), across(u, 2)
        (own,) = project([u], [swap(v)])
        ux, vy, own = lax.optimization_barrier((ux, vy, own))
        vy = swap(vy)
        ud, vd = lax.optimization_barrier((across(ux, 2), across(vy, 1)))
        vx, uy = lax.optimization_barrier((vx, uy))
        px, py = project([ux, uy], [swap(vx), vy], after=[own])
        px, py = across(px, 1), across(py, 2)
        (far_here,) = project([ud], [vd])
        far = across(far_here, 3)
    else:
        blocks = list(project([u], [swap(v)]))
        for j in range(1, n):
            (p,) = project([across(u, j)], [swap(across(v, j))])
            blocks.append(across(p, j))
    message = shape((size + EXT, LANES), bf16)

    def send(kernel, ins, outs, **kw):
        def run(*refs):
            kernel(*refs, **kw)

        return call(run, s, ins, [full(a) for a in ins], outs, [full(a) for a in outs])

    inner = 2 * wide * n_head
    out = [shape((rows, 2 * cols), bf16)]
    if n == 4:

        def over(a, roles):
            pairs = [
                ((2 * c + core) * n + h, (2 * c + core) * n + (h ^ 2))
                for c in range(n) for core in range(2) for h in range(n) if c ^ h in roles
            ]
            return lax.ppermute(a, BOTH, pairs)

        (got1,) = send(give_kernel, (px, py, squares), [message])
        got1 = along(got1, 1)
        (got2,) = send(give_kernel, (far, own), [p_shape])
        (sum1,) = send(join_kernel, (py, px, got1, squares, got1, got2), [message])
        sum1 = over(sum1, (0, 3))
        got2 = along(got2, 1)
        (sum2,) = send(join_kernel, (own, far, got2, squares, got1), [message])
        sum2 = over(sum2, (1, 2))
        ins = (own, px, py, far, got1, got2, sum1, sum2, squares)
        return send(last_kernel, ins, out, inner=inner)[0]
    steps = range(1, n)
    got = send(choose_kernel, (*blocks, squares), [message] * (n - 1), steps=steps)
    got = [along(a, m) for a, m in zip(got, steps)]
    return send(sum_kernel, (*blocks, squares, *got), out, inner=inner)[0]


def solution(mesh):
    n, n_head = mesh.shape["seq"] // 2, mesh.shape["head"]
    assert n == n_head and n & (n - 1) == 0
    in_specs = (
        P("seq", "head"),
        P("seq", "head"),
        P("seq", None),
        P("seq", None),
        P("head", "seq"),
        P("head", "seq"),
        P("head"),
        P("head"),
        P("head", "seq"),
    )

    def run(*args):
        return body(n, n_head, *args)

    return jax.shard_map(run, mesh=mesh, in_specs=in_specs, out_specs=P("seq", "head"), check_vma=False)
```

```python
import jax
import jax.numpy as jnp
from jax import lax
from jax.experimental import pallas as pl
from jax.experimental.pallas import tpu as pltpu
from jax.sharding import PartitionSpec as P

BOTH = ("seq", "head")
HIGH = lax.Precision.HIGHEST
f32, bf16 = jnp.float32, jnp.bfloat16
EXT = 16
LANES = 128
MIB = 1024 * 1024


def call(kernel, scalars, ins, in_specs, outs, out_specs, scratch=(), flops=0, limit=24):
    moved = sum(a.size * a.dtype.itemsize for a in ins) + sum(
        o.size * o.dtype.itemsize for o in outs
    )
    return pl.pallas_call(
        kernel,
        out_shape=outs,
        grid_spec=pltpu.PrefetchScalarGridSpec(
            num_scalar_prefetch=1,
            grid=(1,),
            in_specs=in_specs,
            out_specs=out_specs,
            scratch_shapes=scratch,
        ),
        cost_estimate=pl.CostEstimate(flops=flops, bytes_accessed=moved, transcendentals=0),
        compiler_params=pltpu.CompilerParams(vmem_limit_bytes=limit * MIB),
    )(scalars, *ins)


def full(a):
    return pl.BlockSpec(memory_space=pltpu.VMEM)


def shape(dims, kind):
    return jax.ShapeDtypeStruct(dims, kind)


def nn(a, b, precision=None):
    return jnp.dot(a, b, preferred_element_type=f32, precision=precision)


def nt(a, b, precision=None):
    return lax.dot_general(a, b, (((1,), (1,)), ((), ())), preferred_element_type=f32, precision=precision)


def tn(a, b, precision=None):
    return lax.dot_general(a, b, (((0,), (0,)), ((), ())), preferred_element_type=f32, precision=precision)


def split2(v):
    hi = v.astype(bf16).astype(f32)
    return hi, v - hi


def half_lanes(ref, k):
    n = ref.shape[1] // 2
    return ref[:, pl.ds(pl.multiple_of(k * n, n), n)]


def parts_of(ref, k, rows):
    n = (ref.shape[0] - 2 * rows) // 4
    dt, ld = [jnp.where(k == 0, ref[i : i + n], ref[i + n : i + 2 * n]) for i in (0, 2 * n)]
    b, c = [ref[4 * n + i : 4 * n + i + rows].astype(bf16) for i in (0, rows)]
    return dt, ld, b, c


def channel_map(heads, wide):
    head = lax.broadcasted_iota(jnp.int32, (heads, wide), 0)
    lane = lax.broadcasted_iota(jnp.int32, (heads, wide), 1)
    size = wide // heads
    return ((lane >= head * size) & (lane < (head + 1) * size)).astype(bf16)


def spread(v, spots):
    hi, lo = split2(v)
    return tn(hi.astype(bf16), spots) + tn(lo.astype(bf16), spots)


def ones_upto(rows):
    i = lax.broadcasted_iota(jnp.int32, (rows, rows), 0)
    j = lax.broadcasted_iota(jnp.int32, (rows, rows), 1)
    return (j <= i), (i <= j)


def state_kernel(s, xo, xr, so, sr, msg, first):
    k = s[0]
    rows, wide = xo.shape
    half = pl.ds(pl.multiple_of(k * wide, wide), wide)
    _, upper = ones_upto(rows)
    got = []
    for x, small in ((xo[...], so), (xr[:, half], sr)):
        dt, ld, b, _ = parts_of(small, k, rows)
        spots = channel_map(ld.shape[0], wide)
        run = nn(ld, upper.astype(f32), HIGH)
        last = run[:, rows - 1 :]
        tail = jnp.exp(last - run) * dt
        scaled = (x.astype(f32) * spread(tail, spots)).astype(bf16)
        state = tn(b, scaled)
        decay = spread(jnp.exp(jnp.broadcast_to(last, (last.shape[0], 8))), spots)
        got.append((state, decay))
    (so, do), (sr, dr) = got
    even = k == 0
    s1, s2 = jnp.where(even, so, sr), jnp.where(even, sr, so)
    d2 = jnp.where(even, dr, do)
    n = s1.shape[0]
    flat(msg, (d2[:1] * s1 + s2).astype(bf16))
    msg[wide * n // LANES :] = pair(jnp.concatenate([(do * dr)[:1, i : i + LANES] for i in range(0, wide, LANES)], 0))
    first[...] = s1


def flat(ref, value):
    rows = value.shape[0]
    for i in range(value.shape[1] // LANES):
        ref[i * rows : (i + 1) * rows] = value[:, i * LANES : (i + 1) * LANES]


def pair(v):
    if v.shape[0] < 8:
        v = jnp.concatenate([v, jnp.zeros((8 - v.shape[0], v.shape[1]), f32)], 0)
    hi, lo = split2(v)
    return jnp.concatenate([hi, lo], 0).astype(bf16)


def unpair(v):
    v = v.astype(f32)
    return v[:8] + v[8:]


def unpack(ref, n, wide):
    count = wide // LANES
    state = jnp.concatenate([ref[i * n : (i + 1) * n].astype(f32) for i in range(count)], 1)
    ext = unpair(ref[count * n :])
    return state, jnp.concatenate([ext[i : i + 1] for i in range(count)], 1)


def inside_kernel(s, xo, xr, so, sr, zo, zr, skip, out, decays, gates):
    k = s[0]
    rows, wide = xo.shape
    half = pl.ds(pl.multiple_of(k * wide, wide), wide)
    low, upper = ones_upto(rows)
    count = skip.shape[1] // 2
    gains = jnp.where(k == 0, skip[:, :count], skip[:, count:])
    hi, lo = split2(jnp.broadcast_to(gains, (8, count)))
    spots = channel_map(count, wide)
    gains = nn(hi.astype(bf16), spots) + nn(lo.astype(bf16), spots)
    for turn, (small, z) in enumerate(((so, zo), (sr, zr))):
        start = turn * rows
        dt, ld, b, c = parts_of(small, k, rows)
        heads = ld.shape[0]
        size = wide // heads
        run = nn(ld, upper.astype(f32), HIGH)
        down = nt(low.astype(f32), ld, HIGH)
        decays[start : start + rows] = spread(jnp.exp(run), spots)
        zf = z[:, half].astype(f32)
        gates[start : start + rows] = zf / (1.0 + jnp.exp(-zf))
        scores = jnp.where(low, nt(c, b), 0.0)
        lane = lax.broadcasted_iota(jnp.int32, (rows, 2 * size), 1)
        for pair in range(heads // 2):
            w = []
            for h in (2 * pair, 2 * pair + 1):
                gap = jnp.minimum(down[:, h : h + 1] - run[h : h + 1, :], 0.0)
                w.append((jnp.exp(gap) * scores * dt[h : h + 1, :]).astype(bf16))
            at = slice(2 * pair * size, 2 * (pair + 1) * size)
            if turn == 0:
                xp = xo[:, at]
            else:
                xp = xr[:, pl.ds(pl.multiple_of(k * wide + 2 * pair * size, 2 * size), 2 * size)]
            zero = jnp.zeros_like(xp)
            both = jnp.concatenate([jnp.where(lane < size, xp, zero), jnp.where(lane < size, zero, xp)], 0)
            y = nn(jnp.concatenate(w, 1), both)
            out[start : start + rows, at] = y + gains[:1, at] * xp.astype(f32)


def gate_kernel(s, inside, decays, gates, first, so, sr, gain, _, *rest):
    *states, mine, theirs, sq_mine, sq_theirs = rest
    k = s[0]
    rows, wide = mine.shape
    even = k == 0
    enter, through = None, None
    for j, ref in enumerate(states):
        st, dec = unpack(ref, first.shape[0], wide)
        st = jnp.where(s[2] > j, st, 0.0)
        enter = st if enter is None else enter + st * through
        through = dec if through is None else through * dec
    whole = jnp.where(even, decays[rows - 1 : rows], decays[2 * rows - 1 : 2 * rows])
    second = whole * enter + first[...]
    ones = jnp.ones((8, wide), bf16)
    for turn, (small, out, sq) in enumerate(((so, mine, sq_mine), (sr, theirs, sq_theirs))):
        at = slice(turn * rows, (turn + 1) * rows)
        e = jnp.where(even, enter, second) if turn == 0 else jnp.where(even, second, enter)
        y = inside[at] + nn(parts_of(small, k, rows)[3], e.astype(bf16)) * decays[at]
        gated = y * gates[at]
        hi, lo = split2(gated * gated)
        sq[...] = nt(ones, hi.astype(bf16)) + nt(ones, lo.astype(bf16))
        out[...] = (gated * half_lanes(gain, k)).astype(bf16)


def project_kernel(s, *refs, count, extra):
    u, v = refs[:count], refs[count : 2 * count]
    w_own, w_other = refs[2 * count : 2 * count + 2]
    outs = refs[2 * count + 2 + extra :]
    k = s[0]
    rows, depth = u[0].shape
    cols = w_own.shape[1]
    groups = cols // LANES
    here = pl.ds(pl.multiple_of(k * depth, depth), depth)
    there = pl.ds(pl.multiple_of((1 - k) * depth, depth), depth)
    uu = jnp.concatenate([a[...] for a in u], 0)
    vv = jnp.concatenate([a[...] for a in v], 0)
    for w, place in ((w_own, k), (w_other, 1 - k)):
        got = (nn(uu, w[here]) + nn(vv, w[there])).astype(bf16)
        for i, out in enumerate(outs):
            for j in range(groups):
                at = pl.ds(pl.multiple_of((place * groups + j) * rows, rows), rows)
                out[at] = got[i * rows : (i + 1) * rows, j * LANES : (j + 1) * LANES]


def pick(s, m, blocks, do):
    for j, block in enumerate(blocks):

        @pl.when((s[1] ^ m) == j)
        def _():
            do(block)


def choose_kernel(s, *refs, steps):
    blocks, squares, outs = refs[:-1 - len(steps)], refs[-1 - len(steps)], refs[-len(steps) :]
    n = blocks[0].shape[0]
    for m, out in zip(steps, outs):

        def copy(block, out=out):
            out[:n] = block[...]

        pick(s, m, blocks, copy)
        out[n:] = pair(squares[...])


def give_kernel(s, even, odd, *refs):
    out = refs[-1]
    n = even.shape[0]
    out[:n] = jnp.where((s[1] & 1) == 0, even[...], odd[...])
    if out.shape[0] > n:
        out[n:] = pair(refs[0][...])


def join_kernel(s, even, odd, got, squares, ext, *rest):
    out = rest[-1]
    n = even.shape[0]
    kept = jnp.where((s[1] & 1) == 0, even[...], odd[...])
    out[:n] = (kept.astype(f32) + got[:n].astype(f32)).astype(bf16)
    out[n:] = pair(squares[...] + unpair(ext[n:]))


def row_scale(total, inner, rows):
    i = lax.broadcasted_iota(jnp.int32, (rows, rows), 0)
    j = lax.broadcasted_iota(jnp.int32, (rows, rows), 1)
    row = lax.rsqrt(total[:1] / inner + 1e-5)
    return jnp.sum(jnp.where(i == j, jnp.broadcast_to(row, (rows, rows)), 0.0), axis=1, keepdims=True)


def sum_kernel(s, *refs, inner):
    count = len(refs) // 2 - 1
    blocks, squares, got, out = refs[: count + 1], refs[count + 1], refs[count + 2 : -1], refs[-1]
    rows = out.shape[0]
    n = blocks[0].shape[0]
    col = row_scale(squares[...] + sum(unpair(a[n:]) for a in got), inner, rows)

    def finish(block):
        for g in range(n // rows):
            at = slice(g * rows, (g + 1) * rows)
            v = block[at].astype(f32) + sum(a[at].astype(f32) for a in got)
            out[:, g * LANES : (g + 1) * LANES] = (v * col).astype(bf16)

    pick(s, 0, blocks, finish)


def last_kernel(s, own, x, y, far, got1, got2, sum1, sum2, squares, out, *, inner):
    rows = out.shape[0]
    n = own.shape[0]
    base = squares[...] + unpair(got1[n:])

    def finish(block, got, other):
        col = row_scale(base + unpair(other[n:]), inner, rows)
        for g in range(n // rows):
            at = slice(g * rows, (g + 1) * rows)
            v = block[at].astype(f32) + got[at].astype(f32) + other[at].astype(f32)
            out[:, g * LANES : (g + 1) * LANES] = (v * col).astype(bf16)

    for turn, args in enumerate(((own, got2, sum2), (x, got1, sum1), (y, got1, sum1), (far, got2, sum2))):

        @pl.when(s[1] == turn)
        def _():
            finish(*args)


def body(n, n_head, signal, gate_input, state_in, state_out, step_size, log_decay, skip_gain, norm_gain, out_weight):
    rows = signal.shape[0]
    heads = log_decay.shape[0]
    wide = signal.shape[1] // 2
    states = state_in.shape[1]
    cols = out_weight.shape[1]
    place, z = lax.axis_index("seq"), lax.axis_index("head")
    k, chip = place % 2, place // 2
    s = jnp.stack([k, chip ^ z, chip]).astype(jnp.int32)
    any_spec = pl.BlockSpec(memory_space=pl.ANY)

    def swap(a):
        return lax.ppermute(a, "seq", [(i, i ^ 1) for i in range(2 * n)])

    def across(a, j):
        return lax.ppermute(a, "seq", [(i, i ^ (2 * j)) for i in range(2 * n)])

    def along(a, m):
        return lax.ppermute(a, "head", [(i, i ^ m) for i in range(n)])

    x2 = swap(signal)
    parts = (step_size, log_decay, state_in.astype(f32), state_out.astype(f32))
    tall = sum(a.shape[0] for a in parts)
    at, small1 = 0, 0.0
    for a in parts:
        small1 = small1 + jnp.pad(a, ((at, tall - at - a.shape[0]), (0, 0)))
        at += a.shape[0]
    small2 = swap(small1)
    z2 = swap(gate_input)
    x1 = lax.dynamic_slice_in_dim(signal, k * wide, wide, 1)
    skip = skip_gain.reshape(1, heads)
    gain = norm_gain.reshape(1, 2 * wide)

    ins = (x1, x2, small1, small2)
    outs = [shape((states * wide // LANES + EXT, LANES), bf16), shape((states, wide), f32)]
    msg, first = call(state_kernel, s, ins, [full(a) for a in ins], outs, [full(a) for a in outs])
    w2 = swap(lax.optimization_barrier((out_weight, msg))[0])
    got = [
        lax.ppermute(msg, "seq", [(i, (i + 2 * j) % (2 * n)) for i in range(2 * n)]) for j in range(1, n)
    ]
    ins = (x1, x2, small1, small2, gate_input, z2, skip)
    big = shape((2 * rows, wide), f32)
    inside, decays, gates = call(
        inside_kernel, s, ins, [full(a) for a in ins], [big] * 3, [full(big)] * 3
    )
    ins = (inside, decays, gates, first, small1, small2, gain, w2, *got)
    specs = [full(a) for a in ins[:7]] + [any_spec] + [full(a) for a in got]
    outs = [shape((rows, wide), bf16)] * 2 + [shape((8, rows), f32)] * 2
    u, v, sq_mine, sq_theirs = call(gate_kernel, s, ins, specs, outs, [full(a) for a in outs])
    v = swap(v)
    squares = sq_mine + swap(sq_theirs)

    size = 2 * cols // LANES * rows
    p_shape = shape((size, LANES), bf16)

    def project(u, v, after=(), flops=0):
        ins = (*u, *v, out_weight, w2, *after)
        specs = [full(a) for a in ins[: len(ins) - len(after)]] + [any_spec] * len(after)

        def kernel(*refs):
            project_kernel(*refs, count=len(u), extra=len(after))

        return call(kernel, s, ins, specs, [p_shape] * len(u), [full(p_shape)] * len(u), flops=flops)

    if n == 4:
        ux, vy = across(u, 1), across(v, 2)
        uy, vx = across(u, 2), across(v, 1)
        (own,) = project([u], [v])
        ux, vy, own = lax.optimization_barrier((ux, vy, own))
        ud, vd = lax.optimization_barrier((across(ux, 2), across(vy, 1)))
        px, py = project([ux, uy], [vx, vy], after=[own])
        px, py = across(px, 1), across(py, 2)
        (far_here,) = project([ud], [vd])
        far = across(far_here, 3)
    else:
        blocks = list(project([u], [v]))
        for j in range(1, n):
            (p,) = project([across(u, j)], [across(v, j)])
            blocks.append(across(p, j))
    message = shape((size + EXT, LANES), bf16)

    def send(kernel, ins, outs, **kw):
        def run(*refs):
            kernel(*refs, **kw)

        return call(run, s, ins, [full(a) for a in ins], outs, [full(a) for a in outs])

    inner = 2 * wide * n_head
    out = [shape((rows, 2 * cols), bf16)]
    if n == 4:

        def over(a, ring):
            after = dict(zip(ring, ring[1:] + ring[:1]))
            pairs = []
            for c in range(n):
                for core in range(2):
                    for h in range(n):
                        place = (2 * c + core) * n
                        pairs.append((place + h, place + (c ^ after[c ^ h])))
            return lax.ppermute(a, BOTH, pairs)

        (got1,) = send(give_kernel, (px, py, squares), [message])
        got1 = along(got1, 1)
        (got2,) = send(give_kernel, (far, own), [p_shape])
        (sum1,) = send(join_kernel, (py, px, got1, squares, got1, got2), [message])
        sum1 = over(sum1, (0, 2, 3, 1))
        got2 = along(got2, 1)
        (sum2,) = send(join_kernel, (own, far, got2, squares, got1), [message])
        sum2 = over(sum2, (2, 0, 1, 3))
        ins = (own, px, py, far, got1, got2, sum1, sum2, squares)
        return send(last_kernel, ins, out, inner=inner)[0]
    steps = range(1, n)
    got = send(choose_kernel, (*blocks, squares), [message] * (n - 1), steps=steps)
    got = [along(a, m) for a, m in zip(got, steps)]
    return send(sum_kernel, (*blocks, squares, *got), out, inner=inner)[0]


def solution(mesh):
    n, n_head = mesh.shape["seq"] // 2, mesh.shape["head"]
    assert n == n_head and n & (n - 1) == 0
    in_specs = (
        P("seq", "head"),
        P("seq", "head"),
        P("seq", None),
        P("seq", None),
        P("head", "seq"),
        P("head", "seq"),
        P("head"),
        P("head"),
        P("head", "seq"),
    )

    def run(*args):
        return body(n, n_head, *args)

    return jax.shard_map(run, mesh=mesh, in_specs=in_specs, out_specs=P("seq", "head"), check_vma=False)
```

```python
import jax
import jax.numpy as jnp
from jax import lax
from jax.experimental import pallas as pl
from jax.experimental.pallas import tpu as pltpu
from jax.sharding import PartitionSpec as P

BOTH = ("seq", "head")
HIGH = lax.Precision.HIGHEST
f32, bf16 = jnp.float32, jnp.bfloat16
EXT = 16
LANES = 128
HEAD_ROWS = 16
HEAD_DIM = 64
MIB = 1024 * 1024


def call(kernel, scalars, ins, in_specs, outs, out_specs, scratch=(), flops=0, limit=24):
    moved = sum(a.size * a.dtype.itemsize for a in ins) + sum(
        o.size * o.dtype.itemsize for o in outs
    )
    return pl.pallas_call(
        kernel,
        out_shape=outs,
        grid_spec=pltpu.PrefetchScalarGridSpec(
            num_scalar_prefetch=1,
            grid=(1,),
            in_specs=in_specs,
            out_specs=out_specs,
            scratch_shapes=scratch,
        ),
        cost_estimate=pl.CostEstimate(flops=flops, bytes_accessed=moved, transcendentals=0),
        compiler_params=pltpu.CompilerParams(vmem_limit_bytes=limit * MIB),
    )(scalars, *ins)


def full(a):
    return pl.BlockSpec(memory_space=pltpu.VMEM)


def shape(dims, kind):
    return jax.ShapeDtypeStruct(dims, kind)


def nn(a, b, precision=None):
    return jnp.dot(a, b, preferred_element_type=f32, precision=precision)


def nt(a, b, precision=None):
    return lax.dot_general(a, b, (((1,), (1,)), ((), ())), preferred_element_type=f32, precision=precision)


def tn(a, b, precision=None):
    return lax.dot_general(a, b, (((0,), (0,)), ((), ())), preferred_element_type=f32, precision=precision)


def split2(v):
    hi = v.astype(bf16).astype(f32)
    return hi, v - hi


def half_lanes(ref, k):
    n = ref.shape[1] // 2
    return ref[:, pl.ds(pl.multiple_of(k * n, n), n)]


def parts_of(ref, k, rows):
    n = HEAD_ROWS
    dt, ld = [jnp.where(k == 0, ref[i : i + n], ref[i + n : i + 2 * n]) for i in (0, 2 * n)]
    b, c = [ref[4 * n + i : 4 * n + i + rows].astype(bf16) for i in (0, rows)]
    return dt, ld, b, c


def channel_map(heads, wide):
    head = lax.broadcasted_iota(jnp.int32, (heads, wide), 0)
    lane = lax.broadcasted_iota(jnp.int32, (heads, wide), 1)
    size = HEAD_DIM
    return ((lane >= head * size) & (lane < (head + 1) * size)).astype(bf16)


def spread(v, spots):
    hi, lo = split2(v)
    return tn(jnp.concatenate([hi, lo], 0).astype(bf16), jnp.concatenate([spots, spots], 0))


def sums(v, upper):
    hi, rest = split2(v)
    mid, low = split2(rest)
    n = v.shape[0]
    got = nn(jnp.concatenate([hi, mid, low], 0).astype(bf16), upper.astype(bf16))
    return got[:n] + got[n : 2 * n] + got[2 * n :]


def ones_upto(rows):
    i = lax.broadcasted_iota(jnp.int32, (rows, rows), 0)
    j = lax.broadcasted_iota(jnp.int32, (rows, rows), 1)
    return (j <= i), (i <= j)


def state_kernel(s, xo, xr, so, sr, msg, first):
    k = s[0]
    rows, wide = xo.shape
    half = pl.ds(pl.multiple_of(k * wide, wide), wide)
    _, upper = ones_upto(rows)
    even = k == 0
    own, other = parts_of(so, k, rows), parts_of(sr, k, rows)
    runs = sums(jnp.concatenate([own[1], other[1]], 0), upper)
    lasts = runs[:, rows - 1 :]
    tails = jnp.exp(lasts - runs) * jnp.concatenate([own[0], other[0]], 0)
    n = HEAD_ROWS
    tails = jnp.concatenate([tails[:n], tails[n:]], 1)
    lasts = jnp.broadcast_to(jnp.exp(lasts), (2 * n, LANES))
    spots = channel_map(n, wide)
    wide_tails = spread(tails, spots)
    do, dr = spread(lasts[:n, :8], spots), spread(lasts[n:, :8], spots)
    st_own = tn(own[2], (xo[...].astype(f32) * wide_tails[:rows]).astype(bf16))
    st_other = tn(other[2], (xr[:, half].astype(f32) * wide_tails[rows:]).astype(bf16))
    s1, s2 = jnp.where(even, st_own, st_other), jnp.where(even, st_other, st_own)
    d2 = jnp.where(even, dr, do)
    n = s1.shape[0]
    flat(msg, (d2[:1] * s1 + s2).astype(bf16))
    msg[wide * n // LANES :] = pair(jnp.concatenate([(do * dr)[:1, i : i + LANES] for i in range(0, wide, LANES)], 0))
    first[...] = s1


def flat(ref, value):
    rows = value.shape[0]
    for i in range(value.shape[1] // LANES):
        ref[i * rows : (i + 1) * rows] = value[:, i * LANES : (i + 1) * LANES]


def pair(v):
    if v.shape[0] < 8:
        v = jnp.concatenate([v, jnp.zeros((8 - v.shape[0], v.shape[1]), f32)], 0)
    hi, lo = split2(v)
    return jnp.concatenate([hi, lo], 0).astype(bf16)


def unpair(v):
    v = v.astype(f32)
    return v[:8] + v[8:]


def unpack(ref, n, wide):
    count = wide // LANES
    state = jnp.concatenate([ref[i * n : (i + 1) * n].astype(f32) for i in range(count)], 1)
    ext = unpair(ref[count * n :])
    return state, jnp.concatenate([ext[i : i + 1] for i in range(count)], 1)


def inside_kernel(s, xo, xr, so, sr, zo, zr, skip, out, decays, whole):
    k = s[0]
    rows, wide = xo.shape
    half = pl.ds(pl.multiple_of(k * wide, wide), wide)
    low, upper = ones_upto(rows)
    count = skip.shape[1] // 2
    gains = jnp.where(k == 0, skip[:, :count], skip[:, count:])
    hi, lo = split2(jnp.broadcast_to(gains, (8, count)))
    spots = channel_map(count, wide)
    gains = nn(hi.astype(bf16), spots) + nn(lo.astype(bf16), spots)
    spots = channel_map(HEAD_ROWS, wide)
    for turn, (small, z) in enumerate(((so, zo), (sr, zr))):
        start = turn * rows
        dt, ld, b, c = parts_of(small, k, rows)
        size = HEAD_DIM
        run = sums(ld, upper)
        down = nt(low.astype(f32), ld, HIGH)
        zf = z[:, half].astype(f32)
        gates = zf / (1.0 + jnp.exp(-zf))
        decay = spread(jnp.exp(run), spots)
        decays[start : start + rows] = decay * gates
        whole[8 * turn : 8 * turn + 8] = decay[rows - 8 :]
        scores = jnp.where(low, nt(c, b), 0.0)
        lane = lax.broadcasted_iota(jnp.int32, (rows, 2 * size), 1)
        for duo in range(wide // size // 2):
            w = []
            for h in (2 * duo, 2 * duo + 1):
                gap = jnp.minimum(down[:, h : h + 1] - run[h : h + 1, :], 0.0)
                w.append((jnp.exp(gap) * scores * dt[h : h + 1, :]).astype(bf16))
            at = slice(2 * duo * size, 2 * (duo + 1) * size)
            if turn == 0:
                xp = xo[:, at]
            else:
                xp = xr[:, pl.ds(pl.multiple_of(k * wide + 2 * duo * size, 2 * size), 2 * size)]
            zero = jnp.zeros_like(xp)
            both = jnp.concatenate([jnp.where(lane < size, xp, zero), jnp.where(lane < size, zero, xp)], 0)
            y = nn(jnp.concatenate(w, 1), both)
            out[start : start + rows, at] = (y + gains[:1, at] * xp.astype(f32)) * gates[:, at]


def gate_kernel(s, inside, decays, whole, first, so, sr, gain, _, *rest):
    *states, mine, theirs, sq_mine, sq_theirs = rest
    k = s[0]
    rows, wide = mine.shape
    even = k == 0
    enter, through = None, None
    for j, ref in enumerate(states):
        st, dec = unpack(ref, first.shape[0], wide)
        st = jnp.where(s[2] > j, st, 0.0)
        enter = st if enter is None else enter + st * through
        through = dec if through is None else through * dec
    second = jnp.where(even, whole[7:8], whole[15:16]) * enter + first[...]
    ones = jnp.ones((8, LANES), bf16)
    for turn, (small, out, sq) in enumerate(((so, mine, sq_mine), (sr, theirs, sq_theirs))):
        at = slice(turn * rows, (turn + 1) * rows)
        e = jnp.where(even, enter, second) if turn == 0 else jnp.where(even, second, enter)
        gated = inside[at] + nn(parts_of(small, k, rows)[3], e.astype(bf16)) * decays[at]
        squared = gated * gated
        hi, lo = split2(sum(squared[:, i : i + LANES] for i in range(0, wide, LANES)))
        sq[...] = nt(ones, hi.astype(bf16)) + nt(ones, lo.astype(bf16))
        out[...] = (gated * half_lanes(gain, k)).astype(bf16)


def project_kernel(s, *refs, count, extra):
    u, v = refs[:count], refs[count : 2 * count]
    w_own, w_other = refs[2 * count : 2 * count + 2]
    outs = refs[2 * count + 2 + extra :]
    k = s[0]
    rows, depth = u[0].shape
    cols = w_own.shape[1]
    groups = cols // LANES
    here = pl.ds(pl.multiple_of(k * depth, depth), depth)
    there = pl.ds(pl.multiple_of((1 - k) * depth, depth), depth)
    uu = jnp.concatenate([a[...] for a in u], 0)
    vv = jnp.concatenate([a[...] for a in v], 0)
    for w, place in ((w_own, k), (w_other, 1 - k)):
        got = (nn(uu, w[here]) + nn(vv, w[there])).astype(bf16)
        for i, out in enumerate(outs):
            for j in range(groups):
                at = pl.ds(pl.multiple_of((place * groups + j) * rows, rows), rows)
                out[at] = got[i * rows : (i + 1) * rows, j * LANES : (j + 1) * LANES]


def pick(s, m, blocks, do):
    for j, block in enumerate(blocks):

        @pl.when((s[1] ^ m) == j)
        def _():
            do(block)


def choose_kernel(s, *refs, steps):
    blocks, squares, outs = refs[:-1 - len(steps)], refs[-1 - len(steps)], refs[-len(steps) :]
    n = blocks[0].shape[0]
    for m, out in zip(steps, outs):

        def copy(block, out=out):
            out[:n] = block[...]

        pick(s, m, blocks, copy)
        out[n:] = pair(squares[...])


def give_kernel(s, even, odd, *refs):
    out = refs[-1]
    n = even.shape[0]
    out[:n] = jnp.where((s[1] & 1) == 0, even[...], odd[...])
    if out.shape[0] > n:
        out[n:] = pair(refs[0][...])


def join_kernel(s, even, odd, got, squares, ext, *rest):
    out = rest[-1]
    n = even.shape[0]
    kept = jnp.where((s[1] & 1) == 0, even[...], odd[...])
    out[:n] = (kept.astype(f32) + got[:n].astype(f32)).astype(bf16)
    out[n:] = pair(squares[...] + unpair(ext[n:]))


def row_scale(total, inner, rows):
    i = lax.broadcasted_iota(jnp.int32, (rows, rows), 0)
    j = lax.broadcasted_iota(jnp.int32, (rows, rows), 1)
    row = lax.rsqrt(total[:1] / inner + 1e-5)
    return jnp.sum(jnp.where(i == j, jnp.broadcast_to(row, (rows, rows)), 0.0), axis=1, keepdims=True)


def sum_kernel(s, *refs, inner):
    count = len(refs) // 2 - 1
    blocks, squares, got, out = refs[: count + 1], refs[count + 1], refs[count + 2 : -1], refs[-1]
    rows = out.shape[0]
    n = blocks[0].shape[0]
    col = row_scale(squares[...] + sum(unpair(a[n:]) for a in got), inner, rows)

    def finish(block):
        for g in range(n // rows):
            at = slice(g * rows, (g + 1) * rows)
            v = block[at].astype(f32) + sum(a[at].astype(f32) for a in got)
            out[:, g * LANES : (g + 1) * LANES] = (v * col).astype(bf16)

    pick(s, 0, blocks, finish)


def last_kernel(s, own, x, y, far, got1, got2, sum1, sum2, squares, out, *, inner):
    rows = out.shape[0]
    n = own.shape[0]
    base = squares[...] + unpair(got1[n:])

    def finish(block, got, other):
        col = row_scale(base + unpair(other[n:]), inner, rows)
        for g in range(n // rows):
            at = slice(g * rows, (g + 1) * rows)
            v = block[at].astype(f32) + got[at].astype(f32) + other[at].astype(f32)
            out[:, g * LANES : (g + 1) * LANES] = (v * col).astype(bf16)

    for turn, args in enumerate(((own, got2, sum2), (x, got1, sum1), (y, got1, sum1), (far, got2, sum2))):

        @pl.when(s[1] == turn)
        def _():
            finish(*args)


def body(n, n_head, signal, gate_input, state_in, state_out, step_size, log_decay, skip_gain, norm_gain, out_weight):
    rows = signal.shape[0]
    heads = log_decay.shape[0]
    wide = signal.shape[1] // 2
    states = state_in.shape[1]
    cols = out_weight.shape[1]
    place, z = lax.axis_index("seq"), lax.axis_index("head")
    k, chip = place % 2, place // 2
    s = jnp.stack([k, chip ^ z, chip]).astype(jnp.int32)
    any_spec = pl.BlockSpec(memory_space=pl.ANY)

    def swap(a):
        return lax.ppermute(a, "seq", [(i, i ^ 1) for i in range(2 * n)])

    def across(a, j):
        return lax.ppermute(a, "seq", [(i, i ^ (2 * j)) for i in range(2 * n)])

    def along(a, m):
        return lax.ppermute(a, "head", [(i, i ^ m) for i in range(n)])

    x2 = swap(signal)
    half = heads // 2
    if half == HEAD_ROWS:
        parts, places = [step_size, log_decay], [0, 2 * HEAD_ROWS]
    else:
        parts = [a[i : i + half] for a in (step_size, log_decay) for i in (0, half)]
        places = [i * HEAD_ROWS for i in range(4)]
    parts += [state_in.astype(f32), state_out.astype(f32)]
    places += [4 * HEAD_ROWS, 4 * HEAD_ROWS + rows]
    tall = 4 * HEAD_ROWS + 2 * rows
    small1 = sum(jnp.pad(a, ((at, tall - at - a.shape[0]), (0, 0))) for a, at in zip(parts, places))
    small2 = swap(small1)
    z2 = swap(gate_input)
    x1 = lax.dynamic_slice_in_dim(signal, k * wide, wide, 1)
    skip = skip_gain.reshape(1, heads)
    gain = norm_gain.reshape(1, 2 * wide)

    ins = (x1, x2, small1, small2)
    outs = [shape((states * wide // LANES + EXT, LANES), bf16), shape((states, wide), f32)]
    msg, first = call(state_kernel, s, ins, [full(a) for a in ins], outs, [full(a) for a in outs])
    w2 = swap(lax.optimization_barrier((out_weight, msg))[0])
    got = [
        lax.ppermute(msg, "seq", [(i, (i + 2 * j) % (2 * n)) for i in range(2 * n)]) for j in range(n - 1, 0, -1)
    ][::-1]
    ins = (x1, x2, small1, small2, gate_input, z2, skip)
    big, ends = shape((2 * rows, wide), f32), shape((16, wide), f32)
    inside, decays, whole = call(
        inside_kernel, s, ins, [full(a) for a in ins], [big, big, ends], [full(big)] * 3
    )
    ins = (inside, decays, whole, first, small1, small2, gain, w2, *got)
    specs = [full(a) for a in ins[:7]] + [any_spec] + [full(a) for a in got]
    outs = [shape((rows, wide), bf16)] * 2 + [shape((8, rows), f32)] * 2
    u, v, sq_mine, sq_theirs = call(gate_kernel, s, ins, specs, outs, [full(a) for a in outs])
    v = swap(v)
    squares = sq_mine + swap(sq_theirs)

    size = 2 * cols // LANES * rows
    p_shape = shape((size, LANES), bf16)

    def project(u, v, after=(), flops=0):
        ins = (*u, *v, out_weight, w2, *after)
        specs = [full(a) for a in ins[: len(ins) - len(after)]] + [any_spec] * len(after)

        def kernel(*refs):
            project_kernel(*refs, count=len(u), extra=len(after))

        return call(kernel, s, ins, specs, [p_shape] * len(u), [full(p_shape)] * len(u), flops=flops)

    if n == 4:
        ux, vy = across(u, 1), across(v, 2)
        uy, vx = across(u, 2), across(v, 1)
        (own,) = project([u], [v])
        ux, vy, own = lax.optimization_barrier((ux, vy, own))
        ud, vd = lax.optimization_barrier((across(ux, 2), across(vy, 1)))
        px, py = project([ux, uy], [vx, vy], after=[own])
        px, py = across(px, 1), across(py, 2)
        (far_here,) = project([ud], [vd])
        far = across(far_here, 3)
    else:
        blocks = list(project([u], [v]))
        for j in range(1, n):
            (p,) = project([across(u, j)], [across(v, j)])
            blocks.append(across(p, j))
    message = shape((size + EXT, LANES), bf16)

    def send(kernel, ins, outs, **kw):
        def run(*refs):
            kernel(*refs, **kw)

        return call(run, s, ins, [full(a) for a in ins], outs, [full(a) for a in outs])

    inner = 2 * wide * n_head
    out = [shape((rows, 2 * cols), bf16)]
    if n == 4:

        def over(a, ring):
            after = dict(zip(ring, ring[1:] + ring[:1]))
            pairs = []
            for c in range(n):
                for core in range(2):
                    for h in range(n):
                        place = (2 * c + core) * n
                        pairs.append((place + h, place + (c ^ after[c ^ h])))
            return lax.ppermute(a, BOTH, pairs)

        (got1,) = send(give_kernel, (px, py, squares), [message])
        got1 = along(got1, 1)
        (got2,) = send(give_kernel, (far, own), [p_shape])
        (sum1,) = send(join_kernel, (py, px, got1, squares, got1, got2), [message])
        sum1 = over(sum1, (0, 2, 3, 1))
        got2 = along(got2, 1)
        (sum2,) = send(join_kernel, (own, far, got2, squares, got1), [message])
        sum2 = over(sum2, (2, 0, 1, 3))
        ins = (own, px, py, far, got1, got2, sum1, sum2, squares)
        return send(last_kernel, ins, out, inner=inner)[0]
    steps = range(1, n)
    got = send(choose_kernel, (*blocks, squares), [message] * (n - 1), steps=steps)
    got = [along(a, m) for a, m in zip(got, steps)]
    return send(sum_kernel, (*blocks, squares, *got), out, inner=inner)[0]


def solution(mesh):
    n, n_head = mesh.shape["seq"] // 2, mesh.shape["head"]
    assert n == n_head and n & (n - 1) == 0
    in_specs = (
        P("seq", "head"),
        P("seq", "head"),
        P("seq", None),
        P("seq", None),
        P("head", "seq"),
        P("head", "seq"),
        P("head"),
        P("head"),
        P("head", "seq"),
    )

    def run(*args):
        return body(n, n_head, *args)

    return jax.shard_map(run, mesh=mesh, in_specs=in_specs, out_specs=P("seq", "head"), check_vma=False)
```

```python
import jax
import jax.numpy as jnp
from jax import lax
from jax.experimental import pallas as pl
from jax.experimental.pallas import tpu as pltpu
from jax.sharding import PartitionSpec as P

HIGH = lax.Precision.HIGHEST
f32, bf16 = jnp.float32, jnp.bfloat16
EXT = 16
LANES = 128
HEAD_ROWS = 16
HEAD_DIM = 64
MIB = 1024 * 1024


def call(kernel, scalars, ins, in_specs, outs, out_specs, scratch=(), flops=0, limit=24):
    moved = sum(a.size * a.dtype.itemsize for a in ins) + sum(
        o.size * o.dtype.itemsize for o in outs
    )
    return pl.pallas_call(
        kernel,
        out_shape=outs,
        grid_spec=pltpu.PrefetchScalarGridSpec(
            num_scalar_prefetch=1,
            grid=(1,),
            in_specs=in_specs,
            out_specs=out_specs,
            scratch_shapes=scratch,
        ),
        cost_estimate=pl.CostEstimate(flops=flops, bytes_accessed=moved, transcendentals=0),
        compiler_params=pltpu.CompilerParams(vmem_limit_bytes=limit * MIB),
    )(scalars, *ins)


def full(a):
    return pl.BlockSpec(memory_space=pltpu.VMEM)


def shape(dims, kind):
    return jax.ShapeDtypeStruct(dims, kind)


def nn(a, b, precision=None):
    return jnp.dot(a, b, preferred_element_type=f32, precision=precision)


def nt(a, b, precision=None):
    return lax.dot_general(a, b, (((1,), (1,)), ((), ())), preferred_element_type=f32, precision=precision)


def tn(a, b, precision=None):
    return lax.dot_general(a, b, (((0,), (0,)), ((), ())), preferred_element_type=f32, precision=precision)


def split2(v):
    hi = v.astype(bf16).astype(f32)
    return hi, v - hi


def half_lanes(ref, k):
    n = ref.shape[1] // 2
    return ref[:, pl.ds(pl.multiple_of(k * n, n), n)]


def parts_of(ref, k, rows):
    n = HEAD_ROWS
    dt, ld = [jnp.where(k == 0, ref[i : i + n], ref[i + n : i + 2 * n]) for i in (0, 2 * n)]
    b, c = [ref[4 * n + i : 4 * n + i + rows].astype(bf16) for i in (0, rows)]
    return dt, ld, b, c


def channel_map(heads, wide):
    head = lax.broadcasted_iota(jnp.int32, (heads, wide), 0)
    lane = lax.broadcasted_iota(jnp.int32, (heads, wide), 1)
    size = HEAD_DIM
    return ((lane >= head * size) & (lane < (head + 1) * size)).astype(bf16)


def spread(v, spots):
    hi, lo = split2(v)
    return tn(jnp.concatenate([hi, lo], 0).astype(bf16), jnp.concatenate([spots, spots], 0))


def sums(v, upper):
    hi, rest = split2(v)
    mid, low = split2(rest)
    n = v.shape[0]
    got = nn(jnp.concatenate([hi, mid, low], 0).astype(bf16), upper.astype(bf16))
    return got[:n] + got[n : 2 * n] + got[2 * n :]


def ones_upto(rows):
    i = lax.broadcasted_iota(jnp.int32, (rows, rows), 0)
    j = lax.broadcasted_iota(jnp.int32, (rows, rows), 1)
    return (j <= i), (i <= j)


def state_kernel(s, xo, xr, so, sr, first, *messages):
    k = s[0]
    rows, wide = xo.shape
    half = pl.ds(pl.multiple_of(k * wide, wide), wide)
    _, upper = ones_upto(rows)
    even = k == 0
    own, other = parts_of(so, k, rows), parts_of(sr, k, rows)
    runs = sums(jnp.concatenate([own[1], other[1]], 0), upper)
    lasts = runs[:, rows - 1 :]
    tails = jnp.exp(lasts - runs) * jnp.concatenate([own[0], other[0]], 0)
    n = HEAD_ROWS
    tails = jnp.concatenate([tails[:n], tails[n:]], 1)
    lasts = jnp.broadcast_to(jnp.exp(lasts), (2 * n, LANES))
    spots = channel_map(n, wide)
    wide_tails = spread(tails, spots)
    do, dr = spread(lasts[:n, :8], spots), spread(lasts[n:, :8], spots)
    st_own = tn(own[2], (xo[...].astype(f32) * wide_tails[:rows]).astype(bf16))
    st_other = tn(other[2], (xr[:, half].astype(f32) * wide_tails[rows:]).astype(bf16))
    s1, s2 = jnp.where(even, st_own, st_other), jnp.where(even, st_other, st_own)
    d2 = jnp.where(even, dr, do)
    write_state(messages, d2[:1] * s1 + s2, (do * dr)[:1])
    first[...] = s1


def write_state(messages, state, decay):
    n, wide = state.shape
    part = wide // len(messages)
    for i, msg in enumerate(messages):
        at = slice(i * part, (i + 1) * part)
        flat(msg, state[:, at].astype(bf16))
        msg[part * n // LANES :] = pair(rows_of(decay[:, at]))


def rows_of(v):
    return jnp.concatenate([v[:, i : i + LANES] for i in range(0, v.shape[1], LANES)], 0)


def group_kernel(s, own, other, out, *, bit, n, wide):
    later = (s[2] >> bit) & 1 == 1
    so, do = unpack(own, n, wide)
    st, dt = unpack(other, n, wide)
    s1, s2 = jnp.where(later, st, so), jnp.where(later, so, st)
    write_state([out], jnp.where(later, do, dt) * s1 + s2, do * dt)


def flat(ref, value):
    rows = value.shape[0]
    for i in range(value.shape[1] // LANES):
        ref[i * rows : (i + 1) * rows] = value[:, i * LANES : (i + 1) * LANES]


def rows_of(v):
    return jnp.concatenate([v[:, i : i + LANES] for i in range(0, v.shape[1], LANES)], 0)


def pair(v):
    if v.shape[0] < 8:
        v = jnp.concatenate([v, jnp.zeros((8 - v.shape[0], v.shape[1]), f32)], 0)
    hi, lo = split2(v)
    return jnp.concatenate([hi, lo], 0).astype(bf16)


def unpair(v):
    v = v.astype(f32)
    return v[:8] + v[8:]


def unpack(ref, n, wide):
    count = wide // LANES
    state = jnp.concatenate([ref[i * n : (i + 1) * n].astype(f32) for i in range(count)], 1)
    ext = unpair(ref[count * n :])
    return state, jnp.concatenate([ext[i : i + 1] for i in range(count)], 1)


def inside_kernel(s, xo, xr, so, sr, zo, zr, skip, out, decays, whole):
    k = s[0]
    rows, wide = xo.shape
    half = pl.ds(pl.multiple_of(k * wide, wide), wide)
    low, upper = ones_upto(rows)
    count = skip.shape[1] // 2
    gains = jnp.where(k == 0, skip[:, :count], skip[:, count:])
    hi, lo = split2(jnp.broadcast_to(gains, (8, count)))
    spots = channel_map(count, wide)
    gains = nn(hi.astype(bf16), spots) + nn(lo.astype(bf16), spots)
    spots = channel_map(HEAD_ROWS, wide)
    for turn, (small, z) in enumerate(((so, zo), (sr, zr))):
        start = turn * rows
        dt, ld, b, c = parts_of(small, k, rows)
        size = HEAD_DIM
        run = sums(ld, upper)
        down = nt(low.astype(f32), ld, HIGH)
        zf = z[:, half].astype(f32)
        gates = zf / (1.0 + jnp.exp(-zf))
        decay = spread(jnp.exp(run), spots)
        decays[start : start + rows] = decay * gates
        whole[8 * turn : 8 * turn + 8] = decay[rows - 8 :]
        scores = jnp.where(low, nt(c, b), 0.0)
        lane = lax.broadcasted_iota(jnp.int32, (rows, 2 * size), 1)
        for duo in range(wide // size // 2):
            w = []
            for h in (2 * duo, 2 * duo + 1):
                gap = jnp.minimum(down[:, h : h + 1] - run[h : h + 1, :], 0.0)
                w.append((jnp.exp(gap) * scores * dt[h : h + 1, :]).astype(bf16))
            at = slice(2 * duo * size, 2 * (duo + 1) * size)
            if turn == 0:
                xp = xo[:, at]
            else:
                xp = xr[:, pl.ds(pl.multiple_of(k * wide + 2 * duo * size, 2 * size), 2 * size)]
            zero = jnp.zeros_like(xp)
            both = jnp.concatenate([jnp.where(lane < size, xp, zero), jnp.where(lane < size, zero, xp)], 0)
            y = nn(jnp.concatenate(w, 1), both)
            out[start : start + rows, at] = (y + gains[:1, at] * xp.astype(f32)) * gates[:, at]


def gate_kernel(s, inside, decays, whole, first, so, sr, gain, _, *rest):
    *states, mine, theirs, sq_mine, sq_theirs = rest
    k = s[0]
    rows, wide = mine.shape
    even = k == 0
    count = len(states) // 2
    enters = []
    for half in (states[:count], states[count:]):
        enter, through = None, None
        for bit, ref in enumerate(half):
            st, dec = unpack(ref, first.shape[0], wide // 2)
            earlier = (s[2] >> bit) & 1 == 1
            st, dec = jnp.where(earlier, st, 0.0), jnp.where(earlier, dec, 1.0)
            enter = st if enter is None else enter + st * through
            through = dec if through is None else through * dec
        enters.append(enter)
    enter = jnp.concatenate(enters, 1)
    second = jnp.where(even, whole[7:8], whole[15:16]) * enter + first[...]
    ones = jnp.ones((8, LANES), bf16)
    for turn, (small, out, sq) in enumerate(((so, mine, sq_mine), (sr, theirs, sq_theirs))):
        at = slice(turn * rows, (turn + 1) * rows)
        e = jnp.where(even, enter, second) if turn == 0 else jnp.where(even, second, enter)
        gated = inside[at] + nn(parts_of(small, k, rows)[3], e.astype(bf16)) * decays[at]
        squared = gated * gated
        hi, lo = split2(sum(squared[:, i : i + LANES] for i in range(0, wide, LANES)))
        sq[...] = nt(ones, hi.astype(bf16)) + nt(ones, lo.astype(bf16))
        out[...] = (gated * half_lanes(gain, k)).astype(bf16)


def project_kernel(s, *refs, count, extra):
    u, v = refs[:count], refs[count : 2 * count]
    w_own, w_other = refs[2 * count : 2 * count + 2]
    outs = refs[2 * count + 2 + extra :]
    k = s[0]
    rows, depth = u[0].shape
    cols = w_own.shape[1]
    groups = cols // LANES
    here = pl.ds(pl.multiple_of(k * depth, depth), depth)
    there = pl.ds(pl.multiple_of((1 - k) * depth, depth), depth)
    uu = jnp.concatenate([a[...] for a in u], 0)
    vv = jnp.concatenate([a[...] for a in v], 0)
    for w, place in ((w_own, k), (w_other, 1 - k)):
        got = (nn(uu, w[here]) + nn(vv, w[there])).astype(bf16)
        for i, out in enumerate(outs):
            for j in range(groups):
                at = pl.ds(pl.multiple_of((place * groups + j) * rows, rows), rows)
                out[at] = got[i * rows : (i + 1) * rows, j * LANES : (j + 1) * LANES]


def pick(s, m, blocks, do):
    for j, block in enumerate(blocks):

        @pl.when((s[1] ^ m) == j)
        def _():
            do(block)


def choose_kernel(s, *refs):
    n = len(refs) // 2
    for m, out in enumerate(refs[n:]):

        def copy(block, out=out):
            out[...] = block[...]

        pick(s, m, refs[:n], copy)


def give_kernel(s, even, odd, squares, out):
    n = even.shape[0]
    out[:n] = jnp.where((s[1] & 1) == 0, even[...], odd[...])
    out[n:] = pair(squares[...])


def row_scale(total, inner, rows):
    i = lax.broadcasted_iota(jnp.int32, (rows, rows), 0)
    j = lax.broadcasted_iota(jnp.int32, (rows, rows), 1)
    row = lax.rsqrt(total[:1] / inner + 1e-5)
    return jnp.sum(jnp.where(i == j, jnp.broadcast_to(row, (rows, rows)), 0.0), axis=1, keepdims=True)


def sum_kernel(s, *refs, inner):
    *blocks, squares, out = refs
    rows = out.shape[0]
    col = row_scale(squares[...], inner, rows)
    for g in range(out.shape[1] // LANES):
        at = slice(g * rows, (g + 1) * rows)
        total = sum(a[at].astype(f32) for a in blocks)
        out[:, g * LANES : (g + 1) * LANES] = (total * col).astype(bf16)


def body(n, n_head, signal, gate_input, state_in, state_out, step_size, log_decay, skip_gain, norm_gain, out_weight):
    rows = signal.shape[0]
    heads = log_decay.shape[0]
    wide = signal.shape[1] // 2
    states = state_in.shape[1]
    cols = out_weight.shape[1]
    place, z = lax.axis_index("seq"), lax.axis_index("head")
    k, chip = place % 2, place // 2
    s = jnp.stack([k, chip ^ z, chip]).astype(jnp.int32)
    any_spec = pl.BlockSpec(memory_space=pl.ANY)

    def swap(a):
        return lax.ppermute(a, "seq", [(i, i ^ 1) for i in range(2 * n)])

    def across(a, j):
        return lax.ppermute(a, "seq", [(i, i ^ (2 * j)) for i in range(2 * n)])

    def along(a, m):
        return lax.ppermute(a, "head", [(i, i ^ m) for i in range(n)])

    x2 = swap(signal)
    half = heads // 2
    if half == HEAD_ROWS:
        parts, places = [step_size, log_decay], [0, 2 * HEAD_ROWS]
    else:
        parts = [a[i : i + half] for a in (step_size, log_decay) for i in (0, half)]
        places = [i * HEAD_ROWS for i in range(4)]
    parts += [state_in.astype(f32), state_out.astype(f32)]
    places += [4 * HEAD_ROWS, 4 * HEAD_ROWS + rows]
    tall = 4 * HEAD_ROWS + 2 * rows
    small1 = sum(jnp.pad(a, ((at, tall - at - a.shape[0]), (0, 0))) for a, at in zip(parts, places))
    small2 = swap(small1)
    z2 = swap(gate_input)
    x1 = lax.dynamic_slice_in_dim(signal, k * wide, wide, 1)
    skip = skip_gain.reshape(1, heads)
    gain = norm_gain.reshape(1, 2 * wide)

    ins = (x1, x2, small1, small2)
    msg_shape = shape((states * wide // 2 // LANES + EXT, LANES), bf16)
    outs = [shape((states, wide), f32), msg_shape, msg_shape]
    first, *msgs = call(state_kernel, s, ins, [full(a) for a in ins], outs, [full(a) for a in outs])
    w2 = swap(lax.optimization_barrier((out_weight, msgs[0]))[0])
    got = [[across(msg, 1)] for msg in msgs]
    ins = (x1, x2, small1, small2, gate_input, z2, skip)
    big, ends = shape((2 * rows, wide), f32), shape((16, wide), f32)
    inside, decays, whole = call(
        inside_kernel, s, ins, [full(a) for a in ins], [big, big, ends], [full(big)] * 3
    )
    for bit in range(1, n.bit_length() - 1):

        def group(*refs, bit=bit - 1):
            group_kernel(*refs[:3], refs[-1], bit=bit, n=states, wide=wide // 2)

        for i, msg in enumerate(msgs):
            ins = (msg, got[i][-1])
            (msgs[i],) = call(group, s, ins, [full(a) for a in ins[:2]] + [any_spec] * len(ins[2:]), [msg_shape], [full(msg_shape)])
            got[i].append(across(msgs[i], 1 << bit))
    got = got[0] + got[1]
    ins = (inside, decays, whole, first, small1, small2, gain, w2, *got)
    specs = [full(a) for a in ins[:7]] + [any_spec] + [full(a) for a in got]
    outs = [shape((rows, wide), bf16)] * 2 + [shape((8, rows), f32)] * 2
    u, v, sq_mine, sq_theirs = call(gate_kernel, s, ins, specs, outs, [full(a) for a in outs])
    v = swap(v)
    squares = sq_mine + swap(sq_theirs)

    size = 2 * cols // LANES * rows
    p_shape = shape((size, LANES), bf16)

    def project(u, v, after=(), flops=0):
        ins = (*u, *v, out_weight, w2, *after)
        specs = [full(a) for a in ins[: len(ins) - len(after)]] + [any_spec] * len(after)

        def kernel(*refs):
            project_kernel(*refs, count=len(u), extra=len(after))

        return call(kernel, s, ins, specs, [p_shape] * len(u), [full(p_shape)] * len(u), flops=flops)

    if n == 4:
        ux, vy = across(u, 1), across(v, 2)
        uy, vx = across(u, 2), across(v, 1)
        (own,) = project([u], [v])
        ux, vy, own = lax.optimization_barrier((ux, vy, own))
        ud, vd = lax.optimization_barrier((across(ux, 2), across(vy, 1)))
        px, py = project([ux, uy], [vx, vy], after=[own])
        px, py = across(px, 1), across(py, 2)
        (far_here,) = project([ud], [vd])
        far = across(far_here, 3)
    else:
        blocks = list(project([u], [v]))
        for j in range(1, n):
            (p,) = project([across(u, j)], [across(v, j)])
            blocks.append(across(p, j))
    def attach(block, squares):
        hi = lax.reduce_precision(squares, 8, 7)
        return jnp.concatenate([block, hi.astype(bf16), (squares - hi).astype(bf16)], 0)

    def cut(message):
        more = message[size:].astype(f32)
        return message[:size], more[:8] + more[8:]

    if n == 4:
        r = chip ^ z
        even = r % 2 == 0
        message = shape((size + EXT, LANES), bf16)
        ins = (px, py, squares)
        (give,) = call(give_kernel, s, ins, [full(a) for a in ins], [message], [full(message)])
        got1, more = cut(along(give, 1))
        got2 = along(jnp.where(even, far, own), 1)
        squares = squares + more
        kept1, kept2 = jnp.where(even, py, px), jnp.where(even, own, far)
        first = kept1.astype(f32) + got1.astype(f32)
        second = kept2.astype(f32) + got2.astype(f32)
        outer = (r == 0) | (r == 3)
        other, more = cut(along(attach(jnp.where(outer, first, second).astype(bf16), squares), 2))
        squares = squares + more
        blocks = (other, jnp.where(outer, kept2, kept1), jnp.where(outer, got2, got1))
    else:
        blocks = call(
            choose_kernel, s, blocks, [full(p_shape)] * n, [p_shape] * n, [full(p_shape)] * n
        )
        blocks = [blocks[0]] + [along(blocks[m], m) for m in range(1, n)]
        for bit in range(n.bit_length() - 1):
            squares = squares + along(squares, 1 << bit)

    def add(*refs):
        sum_kernel(*refs, inner=2 * wide * n_head)

    ins = (*blocks, squares)
    out = shape((rows, 2 * cols), bf16)
    return call(add, s, ins, [full(a) for a in ins], [out], [full(out)])[0]


def solution(mesh):
    n, n_head = mesh.shape["seq"] // 2, mesh.shape["head"]
    assert n == n_head and n & (n - 1) == 0
    in_specs = (
        P("seq", "head"),
        P("seq", "head"),
        P("seq", None),
        P("seq", None),
        P("head", "seq"),
        P("head", "seq"),
        P("head"),
        P("head"),
        P("head", "seq"),
    )

    def run(*args):
        return body(n, n_head, *args)

    return jax.shard_map(run, mesh=mesh, in_specs=in_specs, out_specs=P("seq", "head"), check_vma=False)
```

```python
import jax
import jax.numpy as jnp
from jax import lax
from jax.experimental import pallas as pl
from jax.experimental.pallas import tpu as pltpu
from jax.sharding import PartitionSpec as P

HIGH = lax.Precision.HIGHEST
f32, bf16 = jnp.float32, jnp.bfloat16
EXT = 16
LANES = 128
HEAD_ROWS = 16
HEAD_DIM = 64
MIB = 1024 * 1024


def call(kernel, scalars, ins, in_specs, outs, out_specs, scratch=(), flops=0, limit=24):
    moved = sum(a.size * a.dtype.itemsize for a in ins) + sum(
        o.size * o.dtype.itemsize for o in outs
    )
    return pl.pallas_call(
        kernel,
        out_shape=outs,
        grid_spec=pltpu.PrefetchScalarGridSpec(
            num_scalar_prefetch=1,
            grid=(1,),
            in_specs=in_specs,
            out_specs=out_specs,
            scratch_shapes=scratch,
        ),
        cost_estimate=pl.CostEstimate(flops=flops, bytes_accessed=moved, transcendentals=0),
        compiler_params=pltpu.CompilerParams(vmem_limit_bytes=limit * MIB),
    )(scalars, *ins)


def full(a):
    return pl.BlockSpec(memory_space=pltpu.VMEM)


def shape(dims, kind):
    return jax.ShapeDtypeStruct(dims, kind)


def nn(a, b, precision=None):
    return jnp.dot(a, b, preferred_element_type=f32, precision=precision)


def nt(a, b, precision=None):
    return lax.dot_general(a, b, (((1,), (1,)), ((), ())), preferred_element_type=f32, precision=precision)


def tn(a, b, precision=None):
    return lax.dot_general(a, b, (((0,), (0,)), ((), ())), preferred_element_type=f32, precision=precision)


def split2(v):
    hi = v.astype(bf16).astype(f32)
    return hi, v - hi


def half_lanes(ref, k):
    n = ref.shape[1] // 2
    return ref[:, pl.ds(pl.multiple_of(k * n, n), n)]


def parts_of(ref, k, rows):
    n = HEAD_ROWS
    dt, ld = [jnp.where(k == 0, ref[i : i + n], ref[i + n : i + 2 * n]) for i in (0, 2 * n)]
    b, c = [ref[4 * n + i : 4 * n + i + rows].astype(bf16) for i in (0, rows)]
    return dt, ld, b, c


def channel_map(heads, wide):
    head = lax.broadcasted_iota(jnp.int32, (heads, wide), 0)
    lane = lax.broadcasted_iota(jnp.int32, (heads, wide), 1)
    size = HEAD_DIM
    return ((lane >= head * size) & (lane < (head + 1) * size)).astype(bf16)


def spread(v, spots):
    hi, lo = split2(v)
    return tn(jnp.concatenate([hi, lo], 0).astype(bf16), jnp.concatenate([spots, spots], 0))


def sums(v, upper):
    hi, rest = split2(v)
    mid, low = split2(rest)
    n = v.shape[0]
    got = nn(jnp.concatenate([hi, mid, low], 0).astype(bf16), upper.astype(bf16))
    return got[:n] + got[n : 2 * n] + got[2 * n :]


def ones_upto(rows):
    i = lax.broadcasted_iota(jnp.int32, (rows, rows), 0)
    j = lax.broadcasted_iota(jnp.int32, (rows, rows), 1)
    return (j <= i), (i <= j)


def state_kernel(s, xo, xr, so, sr, first, *messages):
    k = s[0]
    rows, wide = xo.shape
    half = pl.ds(pl.multiple_of(k * wide, wide), wide)
    _, upper = ones_upto(rows)
    even = k == 0
    own, other = parts_of(so, k, rows), parts_of(sr, k, rows)
    runs = sums(jnp.concatenate([own[1], other[1]], 0), upper)
    lasts = runs[:, rows - 1 :]
    tails = jnp.exp(lasts - runs) * jnp.concatenate([own[0], other[0]], 0)
    n = HEAD_ROWS
    tails = jnp.concatenate([tails[:n], tails[n:]], 1)
    lasts = jnp.broadcast_to(jnp.exp(lasts), (2 * n, LANES))
    spots = channel_map(n, wide)
    wide_tails = spread(tails, spots)
    do, dr = spread(lasts[:n, :8], spots), spread(lasts[n:, :8], spots)
    st_own = tn(own[2], (xo[...].astype(f32) * wide_tails[:rows]).astype(bf16))
    st_other = tn(other[2], (xr[:, half].astype(f32) * wide_tails[rows:]).astype(bf16))
    s1, s2 = jnp.where(even, st_own, st_other), jnp.where(even, st_other, st_own)
    d2 = jnp.where(even, dr, do)
    write_state(messages, d2[:1] * s1 + s2, (do * dr)[:1])
    first[...] = s1


def write_state(messages, state, decay):
    n, wide = state.shape
    part = wide // len(messages)
    for i, msg in enumerate(messages):
        at = slice(i * part, (i + 1) * part)
        flat(msg, state[:, at].astype(bf16))
        msg[part * n // LANES :] = pair(rows_of(decay[:, at]))


def rows_of(v):
    return jnp.concatenate([v[:, i : i + LANES] for i in range(0, v.shape[1], LANES)], 0)


def group_kernel(s, own, other, out, *, bit, n, wide):
    later = (s[2] >> bit) & 1 == 1
    so, do = unpack(own, n, wide)
    st, dt = unpack(other, n, wide)
    s1, s2 = jnp.where(later, st, so), jnp.where(later, so, st)
    write_state([out], jnp.where(later, do, dt) * s1 + s2, do * dt)


def flat(ref, value):
    rows = value.shape[0]
    for i in range(value.shape[1] // LANES):
        ref[i * rows : (i + 1) * rows] = value[:, i * LANES : (i + 1) * LANES]


def rows_of(v):
    return jnp.concatenate([v[:, i : i + LANES] for i in range(0, v.shape[1], LANES)], 0)


def pair(v):
    if v.shape[0] < 8:
        v = jnp.concatenate([v, jnp.zeros((8 - v.shape[0], v.shape[1]), f32)], 0)
    hi, lo = split2(v)
    return jnp.concatenate([hi, lo], 0).astype(bf16)


def unpair(v):
    v = v.astype(f32)
    return v[:8] + v[8:]


def unpack(ref, n, wide):
    count = wide // LANES
    state = jnp.concatenate([ref[i * n : (i + 1) * n].astype(f32) for i in range(count)], 1)
    ext = unpair(ref[count * n :])
    return state, jnp.concatenate([ext[i : i + 1] for i in range(count)], 1)


def inside_kernel(s, xo, xr, so, sr, zo, zr, skip, out, decays, whole):
    k = s[0]
    rows, wide = xo.shape
    half = pl.ds(pl.multiple_of(k * wide, wide), wide)
    low, upper = ones_upto(rows)
    count = skip.shape[1] // 2
    gains = jnp.where(k == 0, skip[:, :count], skip[:, count:])
    hi, lo = split2(jnp.broadcast_to(gains, (8, count)))
    spots = channel_map(count, wide)
    gains = nn(hi.astype(bf16), spots) + nn(lo.astype(bf16), spots)
    spots = channel_map(HEAD_ROWS, wide)
    for turn, (small, z) in enumerate(((so, zo), (sr, zr))):
        start = turn * rows
        dt, ld, b, c = parts_of(small, k, rows)
        size = HEAD_DIM
        run = sums(ld, upper)
        down = nt(low.astype(f32), ld, HIGH)
        zf = z[:, half].astype(f32)
        gates = zf / (1.0 + jnp.exp(-zf))
        decay = spread(jnp.exp(run), spots)
        decays[start : start + rows] = decay * gates
        whole[8 * turn : 8 * turn + 8] = decay[rows - 8 :]
        scores = jnp.where(low, nt(c, b), 0.0)
        lane = lax.broadcasted_iota(jnp.int32, (rows, 2 * size), 1)
        for duo in range(wide // size // 2):
            w = []
            for h in (2 * duo, 2 * duo + 1):
                gap = jnp.minimum(down[:, h : h + 1] - run[h : h + 1, :], 0.0)
                w.append((jnp.exp(gap) * scores * dt[h : h + 1, :]).astype(bf16))
            at = slice(2 * duo * size, 2 * (duo + 1) * size)
            if turn == 0:
                xp = xo[:, at]
            else:
                xp = xr[:, pl.ds(pl.multiple_of(k * wide + 2 * duo * size, 2 * size), 2 * size)]
            zero = jnp.zeros_like(xp)
            both = jnp.concatenate([jnp.where(lane < size, xp, zero), jnp.where(lane < size, zero, xp)], 0)
            y = nn(jnp.concatenate(w, 1), both)
            out[start : start + rows, at] = (y + gains[:1, at] * xp.astype(f32)) * gates[:, at]


def gate_kernel(s, inside, decays, whole, first, so, sr, gain, _, *rest):
    *states, mine, theirs, sq_mine, sq_theirs = rest
    k = s[0]
    rows, wide = mine.shape
    even = k == 0
    count = len(states) // 2
    enters = []
    for half in (states[:count], states[count:]):
        enter, through = None, None
        for bit, ref in enumerate(half):
            st, dec = unpack(ref, first.shape[0], wide // 2)
            earlier = (s[2] >> bit) & 1 == 1
            st, dec = jnp.where(earlier, st, 0.0), jnp.where(earlier, dec, 1.0)
            enter = st if enter is None else enter + st * through
            through = dec if through is None else through * dec
        enters.append(enter)
    enter = jnp.concatenate(enters, 1)
    second = jnp.where(even, whole[7:8], whole[15:16]) * enter + first[...]
    ones = jnp.ones((8, LANES), bf16)
    for turn, (small, out, sq) in enumerate(((so, mine, sq_mine), (sr, theirs, sq_theirs))):
        at = slice(turn * rows, (turn + 1) * rows)
        e = jnp.where(even, enter, second) if turn == 0 else jnp.where(even, second, enter)
        gated = inside[at] + nn(parts_of(small, k, rows)[3], e.astype(bf16)) * decays[at]
        squared = gated * gated
        hi, lo = split2(sum(squared[:, i : i + LANES] for i in range(0, wide, LANES)))
        sq[...] = nt(ones, hi.astype(bf16)) + nt(ones, lo.astype(bf16))
        out[...] = (gated * half_lanes(gain, k)).astype(bf16)


def project_kernel(s, *refs, count, extra):
    u, v = refs[:count], refs[count : 2 * count]
    w_own, w_other = refs[2 * count : 2 * count + 2]
    outs = refs[2 * count + 2 + extra :]
    k = s[0]
    rows, depth = u[0].shape
    cols = w_own.shape[1]
    groups = cols // LANES
    here = pl.ds(pl.multiple_of(k * depth, depth), depth)
    there = pl.ds(pl.multiple_of((1 - k) * depth, depth), depth)
    uu = jnp.concatenate([a[...] for a in u], 0)
    vv = jnp.concatenate([a[...] for a in v], 0)
    for w, place in ((w_own, k), (w_other, 1 - k)):
        got = (nn(uu, w[here]) + nn(vv, w[there])).astype(bf16)
        for i, out in enumerate(outs):
            for j in range(groups):
                at = pl.ds(pl.multiple_of((place * groups + j) * rows, rows), rows)
                out[at] = got[i * rows : (i + 1) * rows, j * LANES : (j + 1) * LANES]


def pick(s, m, blocks, do):
    for j, block in enumerate(blocks):

        @pl.when((s[1] ^ m) == j)
        def _():
            do(block)


def choose_kernel(s, *refs):
    n = len(refs) // 2
    for m, out in enumerate(refs[n:]):

        def copy(block, out=out):
            out[...] = block[...]

        pick(s, m, refs[:n], copy)


def give_kernel(s, even, odd, squares, out):
    n = even.shape[0]
    out[:n] = jnp.where((s[1] & 1) == 0, even[...], odd[...])
    out[n:] = pair(squares[...])


def row_scale(total, inner, rows):
    i = lax.broadcasted_iota(jnp.int32, (rows, rows), 0)
    j = lax.broadcasted_iota(jnp.int32, (rows, rows), 1)
    row = lax.rsqrt(total[:1] / inner + 1e-5)
    return jnp.sum(jnp.where(i == j, jnp.broadcast_to(row, (rows, rows)), 0.0), axis=1, keepdims=True)


def sum_kernel(s, *refs, inner):
    *blocks, squares, out = refs
    rows = out.shape[0]
    col = row_scale(squares[...], inner, rows)
    for g in range(out.shape[1] // LANES):
        at = slice(g * rows, (g + 1) * rows)
        total = sum(a[at].astype(f32) for a in blocks)
        out[:, g * LANES : (g + 1) * LANES] = (total * col).astype(bf16)


def body(n, n_head, signal, gate_input, state_in, state_out, step_size, log_decay, skip_gain, norm_gain, out_weight):
    rows = signal.shape[0]
    heads = log_decay.shape[0]
    wide = signal.shape[1] // 2
    states = state_in.shape[1]
    cols = out_weight.shape[1]
    place, z = lax.axis_index("seq"), lax.axis_index("head")
    k, chip = place % 2, place // 2
    s = jnp.stack([k, chip ^ z, chip]).astype(jnp.int32)
    any_spec = pl.BlockSpec(memory_space=pl.ANY)

    def swap(a):
        return lax.ppermute(a, "seq", [(i, i ^ 1) for i in range(2 * n)])

    def across(a, j):
        return lax.ppermute(a, "seq", [(i, i ^ (2 * j)) for i in range(2 * n)])

    def along(a, m):
        return lax.ppermute(a, "head", [(i, i ^ m) for i in range(n)])

    x2 = swap(signal)
    half = heads // 2
    if half == HEAD_ROWS:
        parts, places = [step_size, log_decay], [0, 2 * HEAD_ROWS]
    else:
        parts = [a[i : i + half] for a in (step_size, log_decay) for i in (0, half)]
        places = [i * HEAD_ROWS for i in range(4)]
    parts += [state_in.astype(f32), state_out.astype(f32)]
    places += [4 * HEAD_ROWS, 4 * HEAD_ROWS + rows]
    tall = 4 * HEAD_ROWS + 2 * rows
    small1 = sum(jnp.pad(a, ((at, tall - at - a.shape[0]), (0, 0))) for a, at in zip(parts, places))
    small2 = swap(small1)
    z2 = swap(gate_input)
    x1 = lax.dynamic_slice_in_dim(signal, k * wide, wide, 1)
    skip = skip_gain.reshape(1, heads)
    gain = norm_gain.reshape(1, 2 * wide)

    ins = (x1, x2, small1, small2)
    msg_shape = shape((states * wide // 2 // LANES + EXT, LANES), bf16)
    outs = [shape((states, wide), f32), msg_shape, msg_shape]
    first, *msgs = call(state_kernel, s, ins, [full(a) for a in ins], outs, [full(a) for a in outs])
    w2 = swap(lax.optimization_barrier((out_weight, msgs[0]))[0])
    got = [[across(msg, 1)] for msg in msgs]
    ins = (x1, x2, small1, small2, gate_input, z2, skip)
    big, ends = shape((2 * rows, wide), f32), shape((16, wide), f32)
    inside, decays, whole = call(
        inside_kernel, s, ins, [full(a) for a in ins], [big, big, ends], [full(big)] * 3
    )
    for bit in range(1, n.bit_length() - 1):

        def group(*refs, bit=bit - 1):
            group_kernel(*refs[:3], refs[-1], bit=bit, n=states, wide=wide // 2)

        for i, msg in enumerate(msgs):
            ins = (msg, got[i][-1])
            (msgs[i],) = call(group, s, ins, [full(a) for a in ins[:2]] + [any_spec] * len(ins[2:]), [msg_shape], [full(msg_shape)])
            got[i].append(across(msgs[i], 1 << bit))
    got = got[0] + got[1]
    ins = (inside, decays, whole, first, small1, small2, gain, w2, *got)
    specs = [full(a) for a in ins[:7]] + [any_spec] + [full(a) for a in got]
    outs = [shape((rows, wide), bf16)] * 2 + [shape((8, rows), f32)] * 2
    u, v, sq_mine, sq_theirs = call(gate_kernel, s, ins, specs, outs, [full(a) for a in outs])
    v = swap(v)
    squares = sq_mine + swap(sq_theirs)

    size = 2 * cols // LANES * rows
    p_shape = shape((size, LANES), bf16)

    def project(u, v, after=(), flops=0):
        ins = (*u, *v, out_weight, w2, *after)
        specs = [full(a) for a in ins[: len(ins) - len(after)]] + [any_spec] * len(after)

        def kernel(*refs):
            project_kernel(*refs, count=len(u), extra=len(after))

        return call(kernel, s, ins, specs, [p_shape] * len(u), [full(p_shape)] * len(u), flops=flops)

    if n == 4:
        ux, vy = across(u, 1), across(v, 2)
        uy, vx = across(u, 2), across(v, 1)
        (own,) = project([u], [v], after=[squares])
        ux, vy, own = lax.optimization_barrier((ux, vy, own))
        ud, vd = lax.optimization_barrier((across(ux, 2), across(vy, 1)))
        px, py = project([ux, uy], [vx, vy], after=[own])
        px, py = across(px, 1), across(py, 2)
        (far_here,) = project([ud], [vd])
        far = across(far_here, 3)
    else:
        blocks = list(project([u], [v]))
        for j in range(1, n):
            (p,) = project([across(u, j)], [across(v, j)])
            blocks.append(across(p, j))
    def attach(block, squares):
        hi = lax.reduce_precision(squares, 8, 7)
        return jnp.concatenate([block, hi.astype(bf16), (squares - hi).astype(bf16)], 0)

    def cut(message):
        more = message[size:].astype(f32)
        return message[:size], more[:8] + more[8:]

    if n == 4:
        r = chip ^ z
        even = r % 2 == 0
        message = shape((size + EXT, LANES), bf16)
        ins = (px, own, squares)
        (give,) = call(give_kernel, s, ins, [full(a) for a in ins], [message], [full(message)])
        got1, more = cut(along(give, 1))
        got2 = along(jnp.where(even, far, py), 1)
        squares = squares + more
        kept1, kept2 = jnp.where(even, own, px), jnp.where(even, py, far)
        first = kept1.astype(f32) + got1.astype(f32)
        second = kept2.astype(f32) + got2.astype(f32)
        low = r < 2
        other, more = cut(along(attach(jnp.where(low, second, first).astype(bf16), squares), 2))
        squares = squares + more
        blocks = (other, jnp.where(low, kept1, kept2), jnp.where(low, got1, got2))
    else:
        blocks = call(
            choose_kernel, s, blocks, [full(p_shape)] * n, [p_shape] * n, [full(p_shape)] * n
        )
        blocks = [blocks[0]] + [along(blocks[m], m) for m in range(1, n)]
        for bit in range(n.bit_length() - 1):
            squares = squares + along(squares, 1 << bit)

    def add(*refs):
        sum_kernel(*refs, inner=2 * wide * n_head)

    ins = (*blocks, squares)
    out = shape((rows, 2 * cols), bf16)
    return call(add, s, ins, [full(a) for a in ins], [out], [full(out)])[0]


def solution(mesh):
    n, n_head = mesh.shape["seq"] // 2, mesh.shape["head"]
    assert n == n_head and n & (n - 1) == 0
    in_specs = (
        P("seq", "head"),
        P("seq", "head"),
        P("seq", None),
        P("seq", None),
        P("head", "seq"),
        P("head", "seq"),
        P("head"),
        P("head"),
        P("head", "seq"),
    )

    def run(*args):
        return body(n, n_head, *args)

    return jax.shard_map(run, mesh=mesh, in_specs=in_specs, out_specs=P("seq", "head"), check_vma=False)
```

```python
import jax
import jax.numpy as jnp
from jax import lax
from jax.experimental import pallas as pl
from jax.experimental.pallas import tpu as pltpu
from jax.sharding import PartitionSpec as P

HIGH = lax.Precision.HIGHEST
f32, bf16 = jnp.float32, jnp.bfloat16
EXT = 16
LANES = 128
HEAD_ROWS = 16
HEAD_DIM = 64
MIB = 1024 * 1024


def call(kernel, scalars, ins, in_specs, outs, out_specs, scratch=(), flops=0, limit=24):
    moved = sum(a.size * a.dtype.itemsize for a in ins) + sum(
        o.size * o.dtype.itemsize for o in outs
    )
    return pl.pallas_call(
        kernel,
        out_shape=outs,
        grid_spec=pltpu.PrefetchScalarGridSpec(
            num_scalar_prefetch=1,
            grid=(1,),
            in_specs=in_specs,
            out_specs=out_specs,
            scratch_shapes=scratch,
        ),
        cost_estimate=pl.CostEstimate(flops=flops, bytes_accessed=moved, transcendentals=0),
        compiler_params=pltpu.CompilerParams(vmem_limit_bytes=limit * MIB),
    )(scalars, *ins)


def full(a):
    return pl.BlockSpec(memory_space=pltpu.VMEM)


def shape(dims, kind):
    return jax.ShapeDtypeStruct(dims, kind)


def nn(a, b, precision=None):
    return jnp.dot(a, b, preferred_element_type=f32, precision=precision)


def nt(a, b, precision=None):
    return lax.dot_general(a, b, (((1,), (1,)), ((), ())), preferred_element_type=f32, precision=precision)


def tn(a, b, precision=None):
    return lax.dot_general(a, b, (((0,), (0,)), ((), ())), preferred_element_type=f32, precision=precision)


def split2(v):
    hi = v.astype(bf16).astype(f32)
    return hi, v - hi


def half_lanes(ref, k):
    n = ref.shape[1] // 2
    return ref[:, pl.ds(pl.multiple_of(k * n, n), n)]


def parts_of(ref, k, rows):
    n = HEAD_ROWS
    dt, ld = [jnp.where(k == 0, ref[i : i + n], ref[i + n : i + 2 * n]) for i in (0, 2 * n)]
    b, c = [ref[4 * n + i : 4 * n + i + rows].astype(bf16) for i in (0, rows)]
    return dt, ld, b, c


def channel_map(heads, wide):
    head = lax.broadcasted_iota(jnp.int32, (heads, wide), 0)
    lane = lax.broadcasted_iota(jnp.int32, (heads, wide), 1)
    size = HEAD_DIM
    return ((lane >= head * size) & (lane < (head + 1) * size)).astype(bf16)


def spread(v, spots):
    hi, lo = split2(v)
    return tn(jnp.concatenate([hi, lo], 0).astype(bf16), jnp.concatenate([spots, spots], 0))


def sums(v, upper):
    hi, rest = split2(v)
    mid, low = split2(rest)
    n = v.shape[0]
    got = nn(jnp.concatenate([hi, mid, low], 0).astype(bf16), upper.astype(bf16))
    return got[:n] + got[n : 2 * n] + got[2 * n :]


def ones_upto(rows):
    i = lax.broadcasted_iota(jnp.int32, (rows, rows), 0)
    j = lax.broadcasted_iota(jnp.int32, (rows, rows), 1)
    return (j <= i), (i <= j)


def state_kernel(s, xo, xr, so, sr, first, *messages):
    k = s[0]
    rows, wide = xo.shape
    half = pl.ds(pl.multiple_of(k * wide, wide), wide)
    _, upper = ones_upto(rows)
    even = k == 0
    own, other = parts_of(so, k, rows), parts_of(sr, k, rows)
    runs = sums(jnp.concatenate([own[1], other[1]], 0), upper)
    lasts = runs[:, rows - 1 :]
    tails = jnp.exp(lasts - runs) * jnp.concatenate([own[0], other[0]], 0)
    n = HEAD_ROWS
    tails = jnp.concatenate([tails[:n], tails[n:]], 1)
    lasts = jnp.broadcast_to(jnp.exp(lasts), (2 * n, LANES))
    spots = channel_map(n, wide)
    wide_tails = spread(tails, spots)
    do, dr = spread(lasts[:n, :8], spots), spread(lasts[n:, :8], spots)
    st_own = tn(own[2], (xo[...].astype(f32) * wide_tails[:rows]).astype(bf16))
    st_other = tn(other[2], (xr[:, half].astype(f32) * wide_tails[rows:]).astype(bf16))
    s1, s2 = jnp.where(even, st_own, st_other), jnp.where(even, st_other, st_own)
    d2 = jnp.where(even, dr, do)
    write_state(messages, d2[:1] * s1 + s2, (do * dr)[:1])
    first[...] = s1


def write_state(messages, state, decay):
    n, wide = state.shape
    part = wide // len(messages)
    for i, msg in enumerate(messages):
        at = slice(i * part, (i + 1) * part)
        flat(msg, state[:, at].astype(bf16))
        msg[part * n // LANES :] = pair(rows_of(decay[:, at]))


def rows_of(v):
    return jnp.concatenate([v[:, i : i + LANES] for i in range(0, v.shape[1], LANES)], 0)


def group_kernel(s, own, other, out, *, bit, n, wide):
    later = (s[2] >> bit) & 1 == 1
    so, do = unpack(own, n, wide)
    st, dt = unpack(other, n, wide)
    s1, s2 = jnp.where(later, st, so), jnp.where(later, so, st)
    write_state([out], jnp.where(later, do, dt) * s1 + s2, do * dt)


def flat(ref, value):
    rows = value.shape[0]
    for i in range(value.shape[1] // LANES):
        ref[i * rows : (i + 1) * rows] = value[:, i * LANES : (i + 1) * LANES]


def rows_of(v):
    return jnp.concatenate([v[:, i : i + LANES] for i in range(0, v.shape[1], LANES)], 0)


def pair(v):
    if v.shape[0] < 8:
        v = jnp.concatenate([v, jnp.zeros((8 - v.shape[0], v.shape[1]), f32)], 0)
    hi, lo = split2(v)
    return jnp.concatenate([hi, lo], 0).astype(bf16)


def unpair(v):
    v = v.astype(f32)
    return v[:8] + v[8:]


def unpack(ref, n, wide):
    count = wide // LANES
    state = jnp.concatenate([ref[i * n : (i + 1) * n].astype(f32) for i in range(count)], 1)
    ext = unpair(ref[count * n :])
    return state, jnp.concatenate([ext[i : i + 1] for i in range(count)], 1)


def inside_kernel(s, xo, xr, so, sr, zo, zr, skip, out, decays, whole):
    k = s[0]
    rows, wide = xo.shape
    half = pl.ds(pl.multiple_of(k * wide, wide), wide)
    low, upper = ones_upto(rows)
    count = skip.shape[1] // 2
    gains = jnp.where(k == 0, skip[:, :count], skip[:, count:])
    hi, lo = split2(jnp.broadcast_to(gains, (8, count)))
    spots = channel_map(count, wide)
    gains = nn(hi.astype(bf16), spots) + nn(lo.astype(bf16), spots)
    spots = channel_map(HEAD_ROWS, wide)
    for turn, (small, z) in enumerate(((so, zo), (sr, zr))):
        start = turn * rows
        dt, ld, b, c = parts_of(small, k, rows)
        size = HEAD_DIM
        run = sums(ld, upper)
        down = nt(low.astype(f32), ld, HIGH)
        zf = z[:, half].astype(f32)
        gates = zf / (1.0 + jnp.exp(-zf))
        decay = spread(jnp.exp(run), spots)
        decays[start : start + rows] = decay * gates
        whole[8 * turn : 8 * turn + 8] = decay[rows - 8 :]
        scores = jnp.where(low, nt(c, b), 0.0)
        lane = lax.broadcasted_iota(jnp.int32, (rows, 2 * size), 1)
        for duo in range(wide // size // 2):
            w = []
            for h in (2 * duo, 2 * duo + 1):
                gap = jnp.minimum(down[:, h : h + 1] - run[h : h + 1, :], 0.0)
                w.append((jnp.exp(gap) * scores * dt[h : h + 1, :]).astype(bf16))
            at = slice(2 * duo * size, 2 * (duo + 1) * size)
            if turn == 0:
                xp = xo[:, at]
            else:
                xp = xr[:, pl.ds(pl.multiple_of(k * wide + 2 * duo * size, 2 * size), 2 * size)]
            zero = jnp.zeros_like(xp)
            both = jnp.concatenate([jnp.where(lane < size, xp, zero), jnp.where(lane < size, zero, xp)], 0)
            y = nn(jnp.concatenate(w, 1), both)
            out[start : start + rows, at] = (y + gains[:1, at] * xp.astype(f32)) * gates[:, at]


def gate_kernel(s, inside, decays, whole, first, so, sr, gain, _, *rest):
    *states, mine, theirs, sq_mine, sq_theirs = rest
    k = s[0]
    rows, wide = mine.shape
    even = k == 0
    count = len(states) // 2
    enters = []
    for half in (states[:count], states[count:]):
        enter, through = None, None
        for bit, ref in enumerate(half):
            st, dec = unpack(ref, first.shape[0], wide // 2)
            earlier = (s[2] >> bit) & 1 == 1
            st, dec = jnp.where(earlier, st, 0.0), jnp.where(earlier, dec, 1.0)
            enter = st if enter is None else enter + st * through
            through = dec if through is None else through * dec
        enters.append(enter)
    enter = jnp.concatenate(enters, 1)
    second = jnp.where(even, whole[7:8], whole[15:16]) * enter + first[...]
    ones = jnp.ones((8, LANES), bf16)
    for turn, (small, out, sq) in enumerate(((so, mine, sq_mine), (sr, theirs, sq_theirs))):
        at = slice(turn * rows, (turn + 1) * rows)
        e = jnp.where(even, enter, second) if turn == 0 else jnp.where(even, second, enter)
        gated = inside[at] + nn(parts_of(small, k, rows)[3], e.astype(bf16)) * decays[at]
        squared = gated * gated
        hi, lo = split2(sum(squared[:, i : i + LANES] for i in range(0, wide, LANES)))
        sq[...] = nt(ones, hi.astype(bf16)) + nt(ones, lo.astype(bf16))
        out[...] = (gated * half_lanes(gain, k)).astype(bf16)


def project_kernel(s, *refs, count, extra):
    u, v = refs[:count], refs[count : 2 * count]
    w_own, w_other = refs[2 * count : 2 * count + 2]
    outs = refs[2 * count + 2 + extra :]
    k = s[0]
    rows, depth = u[0].shape
    cols = w_own.shape[1]
    groups = cols // LANES
    here = pl.ds(pl.multiple_of(k * depth, depth), depth)
    there = pl.ds(pl.multiple_of((1 - k) * depth, depth), depth)
    uu = jnp.concatenate([a[...] for a in u], 0)
    vv = jnp.concatenate([a[...] for a in v], 0)
    for w, place in ((w_own, k), (w_other, 1 - k)):
        got = (nn(uu, w[here]) + nn(vv, w[there])).astype(bf16)
        for i, out in enumerate(outs):
            for j in range(groups):
                at = pl.ds(pl.multiple_of((place * groups + j) * rows, rows), rows)
                out[at] = got[i * rows : (i + 1) * rows, j * LANES : (j + 1) * LANES]


def pick(s, m, blocks, do):
    for j, block in enumerate(blocks):

        @pl.when((s[1] ^ m) == j)
        def _():
            do(block)


def choose_kernel(s, *refs):
    n = len(refs) // 2
    for m, out in enumerate(refs[n:]):

        def copy(block, out=out):
            out[...] = block[...]

        pick(s, m, refs[:n], copy)


def give_kernel(s, even, odd, squares, out):
    n = even.shape[0]
    out[:n] = jnp.where((s[1] & 1) == 0, even[...], odd[...])
    out[n:] = pair(squares[...])


def row_scale(total, inner, rows):
    i = lax.broadcasted_iota(jnp.int32, (rows, rows), 0)
    j = lax.broadcasted_iota(jnp.int32, (rows, rows), 1)
    row = lax.rsqrt(total[:1] / inner + 1e-5)
    return jnp.sum(jnp.where(i == j, jnp.broadcast_to(row, (rows, rows)), 0.0), axis=1, keepdims=True)


def sum_kernel(s, *refs, inner):
    *blocks, squares, result, out, sems = refs
    rows = out.shape[0]
    col = row_scale(squares[...], inner, rows)
    copies = []
    for g in range(out.shape[1] // LANES):
        at = slice(g * rows, (g + 1) * rows)
        total = sum(a[at].astype(f32) for a in blocks)
        lanes = pl.ds(g * LANES, LANES)
        out[:, lanes] = (total * col).astype(bf16)
        copies.append(pltpu.make_async_copy(out.at[:, lanes], result.at[:, lanes], sems.at[g]))
        copies[-1].start()
    for copy in copies:
        copy.wait()


def body(n, n_head, signal, gate_input, state_in, state_out, step_size, log_decay, skip_gain, norm_gain, out_weight):
    rows = signal.shape[0]
    heads = log_decay.shape[0]
    wide = signal.shape[1] // 2
    states = state_in.shape[1]
    cols = out_weight.shape[1]
    place, z = lax.axis_index("seq"), lax.axis_index("head")
    k, chip = place % 2, place // 2
    s = jnp.stack([k, chip ^ z, chip]).astype(jnp.int32)
    any_spec = pl.BlockSpec(memory_space=pl.ANY)

    def swap(a):
        return lax.ppermute(a, "seq", [(i, i ^ 1) for i in range(2 * n)])

    def across(a, j):
        return lax.ppermute(a, "seq", [(i, i ^ (2 * j)) for i in range(2 * n)])

    def along(a, m):
        return lax.ppermute(a, "head", [(i, i ^ m) for i in range(n)])

    x2 = swap(signal)
    half = heads // 2
    if half == HEAD_ROWS:
        parts, places = [step_size, log_decay], [0, 2 * HEAD_ROWS]
    else:
        parts = [a[i : i + half] for a in (step_size, log_decay) for i in (0, half)]
        places = [i * HEAD_ROWS for i in range(4)]
    parts += [state_in.astype(f32), state_out.astype(f32)]
    places += [4 * HEAD_ROWS, 4 * HEAD_ROWS + rows]
    tall = 4 * HEAD_ROWS + 2 * rows
    small1 = sum(jnp.pad(a, ((at, tall - at - a.shape[0]), (0, 0))) for a, at in zip(parts, places))
    small2 = swap(small1)
    z2 = swap(gate_input)
    x1 = lax.dynamic_slice_in_dim(signal, k * wide, wide, 1)
    skip = skip_gain.reshape(1, heads)
    gain = norm_gain.reshape(1, 2 * wide)

    ins = (x1, x2, small1, small2)
    msg_shape = shape((states * wide // 2 // LANES + EXT, LANES), bf16)
    outs = [shape((states, wide), f32), msg_shape, msg_shape]
    first, *msgs = call(state_kernel, s, ins, [full(a) for a in ins], outs, [full(a) for a in outs])
    w2 = swap(lax.optimization_barrier((out_weight, msgs[0]))[0])
    got = [[across(msg, 1)] for msg in msgs]
    ins = (x1, x2, small1, small2, gate_input, z2, skip)
    big, ends = shape((2 * rows, wide), f32), shape((16, wide), f32)
    inside, decays, whole = call(
        inside_kernel, s, ins, [full(a) for a in ins], [big, big, ends], [full(big)] * 3
    )
    for bit in range(1, n.bit_length() - 1):

        def group(*refs, bit=bit - 1):
            group_kernel(*refs[:3], refs[-1], bit=bit, n=states, wide=wide // 2)

        for i, msg in enumerate(msgs):
            ins = (msg, got[i][-1])
            (msgs[i],) = call(group, s, ins, [full(a) for a in ins[:2]] + [any_spec] * len(ins[2:]), [msg_shape], [full(msg_shape)])
            got[i].append(across(msgs[i], 1 << bit))
    got = got[0] + got[1]
    ins = (inside, decays, whole, first, small1, small2, gain, w2, *got)
    specs = [full(a) for a in ins[:7]] + [any_spec] + [full(a) for a in got]
    outs = [shape((rows, wide), bf16)] * 2 + [shape((8, rows), f32)] * 2
    u, v, sq_mine, sq_theirs = call(gate_kernel, s, ins, specs, outs, [full(a) for a in outs])
    v = swap(v)
    squares = sq_mine + swap(sq_theirs)

    size = 2 * cols // LANES * rows
    p_shape = shape((size, LANES), bf16)

    def project(u, v, after=(), flops=0):
        ins = (*u, *v, out_weight, w2, *after)
        specs = [full(a) for a in ins[: len(ins) - len(after)]] + [any_spec] * len(after)

        def kernel(*refs):
            project_kernel(*refs, count=len(u), extra=len(after))

        return call(kernel, s, ins, specs, [p_shape] * len(u), [full(p_shape)] * len(u), flops=flops)

    if n == 4:
        ux, vy = across(u, 1), across(v, 2)
        uy, vx = across(u, 2), across(v, 1)
        (own,) = project([u], [v], after=[squares])
        ux, vy, own = lax.optimization_barrier((ux, vy, own))
        ud, vd = lax.optimization_barrier((across(ux, 2), across(vy, 1)))
        px, py = project([ux, uy], [vx, vy], after=[own])
        px, py = across(px, 1), across(py, 2)
        (far_here,) = project([ud], [vd])
        far = across(far_here, 3)
    else:
        blocks = list(project([u], [v]))
        for j in range(1, n):
            (p,) = project([across(u, j)], [across(v, j)])
            blocks.append(across(p, j))
    def attach(block, squares):
        hi = lax.reduce_precision(squares, 8, 7)
        return jnp.concatenate([block, hi.astype(bf16), (squares - hi).astype(bf16)], 0)

    def cut(message):
        more = message[size:].astype(f32)
        return message[:size], more[:8] + more[8:]

    if n == 4:
        r = chip ^ z
        even = r % 2 == 0
        message = shape((size + EXT, LANES), bf16)
        ins = (px, own, squares)
        (give,) = call(give_kernel, s, ins, [full(a) for a in ins], [message], [full(message)])
        got1, more = cut(along(give, 1))
        got2 = along(jnp.where(even, far, py), 1)
        squares = squares + more
        kept1, kept2 = jnp.where(even, own, px), jnp.where(even, py, far)
        first = kept1.astype(f32) + got1.astype(f32)
        second = kept2.astype(f32) + got2.astype(f32)
        low = r < 2
        other, more = cut(along(attach(jnp.where(low, second, first).astype(bf16), squares), 2))
        squares = squares + more
        blocks = (other, jnp.where(low, kept1, kept2), jnp.where(low, got1, got2))
    else:
        blocks = call(
            choose_kernel, s, blocks, [full(p_shape)] * n, [p_shape] * n, [full(p_shape)] * n
        )
        blocks = [blocks[0]] + [along(blocks[m], m) for m in range(1, n)]
        for bit in range(n.bit_length() - 1):
            squares = squares + along(squares, 1 << bit)

    def add(*refs):
        sum_kernel(*refs, inner=2 * wide * n_head)

    ins = (*blocks, squares)
    out = shape((rows, 2 * cols), bf16)
    return call(
        add, s, ins, [full(a) for a in ins], [out], [pl.BlockSpec(memory_space=pl.ANY)],
        scratch=[pltpu.VMEM(out.shape, bf16), pltpu.SemaphoreType.DMA((out.shape[1] // LANES,))],
    )[0]


def solution(mesh):
    n, n_head = mesh.shape["seq"] // 2, mesh.shape["head"]
    assert n == n_head and n & (n - 1) == 0
    in_specs = (
        P("seq", "head"),
        P("seq", "head"),
        P("seq", None),
        P("seq", None),
        P("head", "seq"),
        P("head", "seq"),
        P("head"),
        P("head"),
        P("head", "seq"),
    )

    def run(*args):
        return body(n, n_head, *args)

    return jax.shard_map(run, mesh=mesh, in_specs=in_specs, out_specs=P("seq", "head"), check_vma=False)
```
